32 devices in a mesh: head: 2 (over x), ctx: 16 (over z, y, core).
Axes of the slice: x: 2, y: 2, z: 4, core: 2. Of those that a mesh axis runs over, the one named last changes fastest.
Arguments:
- queries: bfloat16 [8192, 1024], P('ctx', 'head'), may hold values from -26.25 to 26.25
- keys: bfloat16 [8192, 256], P(('ctx', 'head')), may hold values from -7.5 to 7.5
- values: bfloat16 [8192, 256], P(('ctx', 'head')), may hold values from -5 to 5
- selected: int32 [2, 16, 3], P('head'), may hold values from 0 to 15, as said below
Outputs:
- attended: bfloat16 [8192, 1024], P('ctx', 'head')
The draws below stay inside these ranges and needn't reach their ends.
Inputs may be any that keep to these rules, and one draw needn't show every extreme that they name: `selected`: row b of every key-value head holds b in slot 0; its other 2 slots hold distinct blocks below b, or b again where fewer than 2 blocks lie below b.
All inputs are finite; a program needn't handle non-finite values.
Results may differ from the reference program's by a relative error of at most 0.0041.
Values may be sent and summed in bfloat16 or wider, within the bound.
No kernel may reach another device: no remote copies, remote signals or barrier semaphores. Data moves between devices by JAX's collectives and lax.ppermute only.
A program may use at most 64 MiB of HBM per device.

```python
import jax
import jax.numpy as jnp
from jax import lax

HD = 128
QH = 4
BLK = 512
TOPK = 3
KVH = 2
HEADS = 8
TOKENS = 8192
NB = 16


def shared_keys(key):
    base_key = jax.random.fold_in(key, 101)
    drawn = 1.5 * jax.random.truncated_normal(jax.random.fold_in(base_key, 1), -4.0, 4.0, (TOKENS, KVH, HD), jnp.float32)
    return drawn


def draw_keys(key, part):
    mixed = shared_keys(key)
    return mixed.reshape(TOKENS, KVH * HD).astype(jnp.bfloat16)


def draw_queries(key, part):
    drawn = jax.random.truncated_normal(jax.random.fold_in(key, 202), -4.0, 4.0, (TOKENS, HEADS, HD), jnp.float32)
    return drawn.reshape(TOKENS, HEADS * HD).astype(jnp.bfloat16)


def draw_selected(key, part):
    popularity = jax.random.randint(jax.random.fold_in(key, 301), (KVH, 1, NB), 0, 4)
    jitter = jax.random.randint(jax.random.fold_in(key, 302), (KVH, NB, NB), 0, 2 ** 18)
    row_ids = jnp.arange(NB, dtype=jnp.int32)[None, :, None]
    col_ids = jnp.arange(NB, dtype=jnp.int32)[None, None, :]
    earlier = col_ids < row_ids
    ranked = jnp.where(earlier, (jitter + popularity * 2 ** 18) * NB + col_ids, -1 - col_ids)
    picked_score, picked = lax.top_k(ranked, TOPK - 1)
    picked = jnp.where(picked_score >= 0, picked, row_ids)
    own_slot = jnp.broadcast_to(row_ids, (KVH, NB, 1))
    return jnp.concatenate([own_slot, picked.astype(jnp.int32)], axis=2).astype(jnp.int32)


def steps_of(own_key, shape, pieces, low, largest):
    level = 1.0
    for position, blocks in pieces:
        steps = jax.random.uniform(jax.random.fold_in(jax.random.fold_in(own_key, 6), position), (blocks,), jnp.float32, low / len(pieces), largest / len(pieces))
        level = level * jnp.repeat(jnp.exp(steps), shape[position] // blocks).reshape((-1,) + (1,) * (len(shape) - 1 - position))
    return level


def scatter_about(key, dims, scale, bound, split=(), kind=jnp.bfloat16):
    array = scale * jax.random.normal(key, dims, jnp.float32)
    if split:
        array = array * steps_of(key, dims, split, -0.22, 0.18)
    return jnp.clip(array, -bound, bound).astype(kind)


def setup_inputs(seed: int = 0) -> dict:
    seeds = jax.random.split(jax.random.key(seed), 5)
    queries = draw_queries(jax.random.fold_in(seeds[4], 71), 0)
    keys = draw_keys(jax.random.fold_in(seeds[4], 71), 0)
    values = scatter_about(seeds[2], (TOKENS, KVH * HD), 1.0, 5.0, ((0, 32),))
    selected = draw_selected(jax.random.fold_in(seeds[4], 71), 0)
    return {"queries": queries, "keys": keys, "values": values, "selected": selected}


def reference(queries, keys, values, selected):
    blocks_all = TOKENS // BLK
    query_view = queries.reshape(blocks_all, BLK, HEADS, HD)
    key_view = keys.reshape(blocks_all, BLK, KVH, HD)
    value_view = values.reshape(blocks_all, BLK, KVH, HD)
    positions = jnp.arange(BLK, dtype=jnp.int32)
    causal = positions[:, None] >= positions[None, :]
    first_slot = jnp.arange(TOPK, dtype=jnp.int32) == 0
    factor = HD ** -0.5

    def one_pair(pair_index):
        head_id = pair_index // blocks_all
        block_id = pair_index % blocks_all
        group_id = head_id // QH
        chosen = selected[group_id, block_id]
        query_rows = query_view[block_id, :, head_id, :].astype(jnp.float32)
        key_rows = key_view[chosen][:, :, group_id, :].astype(jnp.float32)
        value_rows = value_view[chosen][:, :, group_id, :].astype(jnp.float32)
        scores = jnp.einsum("qd,tkd->qtk", query_rows, key_rows) * factor
        slot_live = first_slot | (chosen != block_id)
        allowed = jnp.where(first_slot[None, :, None], causal[:, None, :], slot_live[None, :, None])
        scores = jnp.where(allowed, scores, -jnp.inf)
        top_score = jnp.max(scores, axis=(1, 2), keepdims=True)
        weights = jnp.exp(scores - top_score)
        weight_sum = jnp.sum(weights, axis=(1, 2))
        rounded = lax.optimization_barrier(weights.astype(jnp.bfloat16)).astype(jnp.float32)
        numerator = jnp.einsum("qtk,tkd->qd", rounded, value_rows)
        return (numerator / weight_sum[:, None]).astype(jnp.bfloat16)

    results = lax.map(one_pair, jnp.arange(HEADS * blocks_all, dtype=jnp.int32))
    results = results.reshape(HEADS, blocks_all, BLK, HD).transpose(1, 2, 0, 3)
    return results.reshape(TOKENS, HEADS * HD)
```

```python
import functools
import math

import jax
import jax.numpy as jnp
from jax import lax
from jax.experimental import pallas as pl
from jax.experimental.pallas import tpu as pltpu
from jax.sharding import PartitionSpec as P

HD = 128
QH = 4
BLK = 512
CHUNK = 256


def pick_kernel(lists_ref, pieces_ref, out_ref):
    receivers, _, picks, parts, rows, _ = out_ref.shape

    def one(receiver, carry):
        for s in range(picks):
            block = lists_ref[receiver, s + 1]
            for part in range(parts):
                for kv in range(2):
                    out_ref[receiver, kv, s, part] = pieces_ref[part, block, kv]
        return carry

    lax.fori_loop(0, receivers, one, 0, unroll=4)


def pick_pieces(lists, pieces, receivers, picks):
    parts, _, _, rows, _ = pieces.shape
    return pl.pallas_call(
        pick_kernel,
        out_shape=jax.ShapeDtypeStruct((receivers, 2, picks, parts, rows, HD), pieces.dtype),
        in_specs=[
            pl.BlockSpec(memory_space=pltpu.SMEM),
            pl.BlockSpec(memory_space=pltpu.VMEM),
        ],
        out_specs=pl.BlockSpec(memory_space=pltpu.VMEM),
    )(lists, pieces)


def scores_of(query_rows, key_rows):
    return lax.dot_general(
        query_rows, key_rows, (((1,), (1,)), ((), ())), preferred_element_type=jnp.float32
    )


def attend_kernel(live_ref, query_ref, own_key_ref, own_value_ref, far_ref, out_ref):
    factor = math.log2(math.e) / math.sqrt(HD)
    picks = far_ref.shape[2]
    far_rows = (BLK, HD)
    far_keys = [far_ref[:, 0, s].reshape(far_rows) for s in range(picks)]
    far_values = [far_ref[:, 1, s].reshape(far_rows) for s in range(picks)]
    for begin in range(0, BLK, CHUNK):
        end = begin + CHUNK
        query_rows = query_ref[begin:end, :]
        near = scores_of(query_rows, own_key_ref[0:end, :])
        row_ids = lax.broadcasted_iota(jnp.int32, near.shape, 0) + begin
        col_ids = lax.broadcasted_iota(jnp.int32, near.shape, 1)
        near = jnp.where(row_ids >= col_ids, near, -jnp.inf)
        pieces = [near]
        for s in range(picks):
            far = scores_of(query_rows, far_keys[s])
            pieces.append(jnp.where(live_ref[s] > 0, far, -jnp.inf))
        top = functools.reduce(
            jnp.maximum, [jnp.max(piece, axis=1, keepdims=True) for piece in pieces]
        )
        weights = [jnp.exp2((piece - top) * factor) for piece in pieces]
        total = sum(jnp.sum(weight, axis=1, keepdims=True) for weight in weights)
        value_parts = [own_value_ref[0:end, :]] + far_values
        product = sum(
            jnp.dot(weight.astype(jnp.bfloat16), value, preferred_element_type=jnp.float32)
            for weight, value in zip(weights, value_parts)
        )
        out_ref[begin:end, :] = (product / total).astype(out_ref.dtype)


def attend(live, queries, own_keys, own_values, far):
    rows, columns = queries.shape
    whole = lambda shape: pl.BlockSpec(shape, lambda h: (0,) * len(shape))
    return pl.pallas_call(
        attend_kernel,
        grid=(columns // HD,),
        out_shape=jax.ShapeDtypeStruct(queries.shape, queries.dtype),
        in_specs=[
            pl.BlockSpec(memory_space=pltpu.SMEM),
            pl.BlockSpec((rows, HD), lambda h: (0, h)),
            whole(own_keys.shape),
            whole(own_values.shape),
            whole(far.shape),
        ],
        out_specs=pl.BlockSpec((rows, HD), lambda h: (0, h)),
        compiler_params=pltpu.CompilerParams(vmem_limit_bytes=48 * 1024 * 1024),
    )(live, queries, own_keys, own_values, far)


def on_device(heads, ranks, queries, keys, values, selected):
    lists = selected[0]
    picks = lists.shape[1] - 1
    head_rank = lax.axis_index("head")
    ctx_rank = lax.axis_index("ctx")
    held = keys.shape[0]
    share = held // ranks

    local = jnp.stack([keys, values]).reshape(2, held, heads, HD)

    by_head = local.transpose(2, 0, 1, 3)
    if heads == 2:
        mine = lax.dynamic_index_in_dim(by_head, head_rank, 0, keepdims=False)
        other = lax.dynamic_index_in_dim(by_head, 1 - head_rank, 0, keepdims=False)
        came = lax.ppermute(other, "head", [(0, 1), (1, 0)])
        own = jnp.where(
            head_rank == 0,
            jnp.concatenate([mine, came], axis=1),
            jnp.concatenate([came, mine], axis=1),
        )
    else:
        own = lax.all_to_all(by_head, "head", split_axis=0, concat_axis=0, tiled=True)
        own = own.transpose(1, 0, 2, 3).reshape(2, BLK, HD)

    spread = local.reshape(2, ranks, share, heads, HD).transpose(3, 1, 0, 2, 4)
    spread = spread.reshape(heads * ranks, 2, share, HD)
    spread = lax.all_to_all(spread, ("head", "ctx"), split_axis=0, concat_axis=0, tiled=True)
    spread = spread.reshape(heads, ranks, 2, share, HD)
    if share % 16:
        spread = spread.transpose(1, 2, 0, 3, 4).reshape(1, ranks, 2, heads * share, HD)

    far = pick_pieces(lists, spread, ranks, picks)
    far = lax.all_to_all(far, "ctx", split_axis=0, concat_axis=0, tiled=True)
    far = far.reshape(ranks, 2, picks, -1, HD)

    chosen = lax.dynamic_index_in_dim(lists, ctx_rank, 0, keepdims=False)[1:]
    live = (chosen != ctx_rank).astype(jnp.int32)
    return attend(live, queries, own[0], own[1], far)


def solution(mesh):
    return jax.shard_map(
        functools.partial(on_device, mesh.shape["head"], mesh.shape["ctx"]),
        mesh=mesh,
        in_specs=(
            P("ctx", "head"),
            P(("ctx", "head"), None),
            P(("ctx", "head"), None),
            P("head", None, None),
        ),
        out_specs=P("ctx", "head"),
        check_vma=False,
    )
```

```python
import functools
import math

import jax
import jax.numpy as jnp
from jax import lax
from jax.experimental import pallas as pl
from jax.experimental.pallas import tpu as pltpu
from jax.sharding import PartitionSpec as P

HD = 128
BLK = 512
CHUNK = 256
FACTOR = math.log2(math.e) / math.sqrt(HD)
SMALL = pltpu.CompilerParams(vmem_limit_bytes=4 * 1024 * 1024)
LARGE = pltpu.CompilerParams(vmem_limit_bytes=24 * 1024 * 1024)
VMEM = pl.BlockSpec(memory_space=pltpu.VMEM)
SMEM = pl.BlockSpec(memory_space=pltpu.SMEM)


def spread_kernel(key_ref, value_ref, out_ref):
    peers, _, share, _ = out_ref.shape
    ranks = key_ref.shape[0] // share
    for kv, ref in enumerate((key_ref, value_ref)):
        for h in range(peers // ranks):
            columns = ref[:, h * HD : (h + 1) * HD]
            out_ref[h * ranks : (h + 1) * ranks, kv] = columns.reshape(ranks, share, HD)


def spread_rows(keys, values, heads, ranks):
    held = keys.shape[0]
    share = held // ranks
    if share % 16 == 0:
        return pl.pallas_call(
            spread_kernel,
            out_shape=jax.ShapeDtypeStruct((heads * ranks, 2, share, HD), keys.dtype),
            in_specs=[VMEM, VMEM],
            out_specs=VMEM,
            compiler_params=SMALL,
        )(keys, values)
    both = jnp.stack([keys, values]).reshape(2, ranks, share, heads, HD)
    return both.transpose(3, 1, 0, 2, 4).reshape(heads * ranks, 2, share, HD)


def pick_kernel(lists_ref, pieces_ref, out_ref):
    receivers, _, picks, parts, _, _ = out_ref.shape

    def one(receiver, carry):
        for s in range(picks):
            block = lists_ref[receiver, s + 1]
            for part in range(parts):
                for kv in range(2):
                    out_ref[receiver, kv, s, part] = pieces_ref[part, block, kv]
        return carry

    lax.fori_loop(0, receivers, one, 0, unroll=4)


def pick_pieces(lists, pieces, receivers, picks):
    parts, _, _, rows, _ = pieces.shape
    return pl.pallas_call(
        pick_kernel,
        out_shape=jax.ShapeDtypeStruct((receivers, 2, picks, parts, rows, HD), pieces.dtype),
        in_specs=[SMEM, VMEM],
        out_specs=VMEM,
        compiler_params=SMALL,
    )(lists, pieces)


def split_queries(query_rows):
    scaled = query_rows.astype(jnp.float32) * FACTOR
    high = scaled.astype(jnp.bfloat16)
    low = (scaled - high.astype(jnp.float32)).astype(jnp.bfloat16)
    return jnp.concatenate([high, low], axis=1)


def units_of(columns):
    return [(h, begin) for h in range(columns // HD) for begin in range(0, BLK, CHUNK)]


def in_turn(units, score, finish):
    held = score(*units[0])
    for i, unit in enumerate(units):
        later = score(*units[i + 1]) if i + 1 < len(units) else None
        finish(*unit, held)
        held = later


def near_kernel(query_ref, key_ref, value_ref, top_ref, sum_ref, acc_ref, turned):
    turned[:HD] = key_ref[...].T
    turned[HD:] = turned[:HD]
    values = jnp.concatenate([value_ref[...], jnp.ones(value_ref.shape, jnp.bfloat16)], axis=1)

    def score(h, begin):
        query_rows = split_queries(query_ref[begin : begin + CHUNK, h * HD : (h + 1) * HD])
        end = begin + CHUNK
        scores = jnp.dot(query_rows, turned[:, :end], preferred_element_type=jnp.float32)
        row_ids = lax.broadcasted_iota(jnp.int32, scores.shape, 0) + begin
        col_ids = lax.broadcasted_iota(jnp.int32, scores.shape, 1)
        return jnp.where(row_ids >= col_ids, scores, -jnp.inf)

    def finish(h, begin, scores):
        rows = slice(begin, begin + CHUNK)
        top = jnp.max(scores, axis=1, keepdims=True)
        weights = jnp.exp2(scores - top).astype(jnp.bfloat16)
        product = jnp.dot(weights, values[: begin + CHUNK], preferred_element_type=jnp.float32)
        top_ref[h, rows] = jnp.broadcast_to(top, (CHUNK, HD))
        sum_ref[h, rows] = product[:, HD:]
        acc_ref[h, rows] = product[:, :HD]

    in_turn(units_of(query_ref.shape[1]), score, finish)


def attend_near(queries, own_keys, own_values):
    rows, columns = queries.shape
    part = jax.ShapeDtypeStruct((columns // HD, rows, HD), jnp.float32)
    return pl.pallas_call(
        near_kernel,
        out_shape=[part, part, part],
        in_specs=[VMEM] * 3,
        out_specs=[VMEM] * 3,
        scratch_shapes=[pltpu.VMEM((2 * HD, BLK), jnp.bfloat16)],
        compiler_params=LARGE,
        cost_estimate=pl.CostEstimate(
            flops=4 * columns * rows * BLK, bytes_accessed=4 << 20, transcendentals=0
        ),
    )(queries, own_keys, own_values)


def far_kernel(
    live_ref, query_ref, key_ref, far_ref, top_ref, sum_ref, acc_ref, out_ref, turned, valued
):
    picks = far_ref.shape[2]
    spare = jnp.broadcast_to(key_ref[0:1, :], (BLK, HD))
    for s in range(picks):
        rows = slice(s * BLK, (s + 1) * BLK)
        live = live_ref[s] > 0
        key_rows = jnp.where(live, far_ref[:, 0, s].reshape(BLK, HD), spare)
        value_rows = far_ref[:, 1, s].reshape(BLK, HD)
        turned[:HD, rows] = key_rows.T
        valued[rows, :HD] = jnp.where(live, value_rows, jnp.zeros_like(value_rows))
        valued[rows, HD:] = jnp.where(
            live, jnp.ones_like(value_rows), jnp.zeros_like(value_rows)
        )
    turned[HD:] = turned[:HD]

    def score(h, begin):
        query_rows = split_queries(query_ref[begin : begin + CHUNK, h * HD : (h + 1) * HD])
        return jnp.dot(query_rows, turned[...], preferred_element_type=jnp.float32)

    def finish(h, begin, scores):
        rows = slice(begin, begin + CHUNK)
        near_top = top_ref[h, rows]
        top = jnp.maximum(jnp.max(scores, axis=1, keepdims=True), near_top[:, :1])
        weights = jnp.exp2(scores - top).astype(jnp.bfloat16)
        product = jnp.dot(weights, valued[...], preferred_element_type=jnp.float32)
        scale = jnp.exp2(near_top - top)
        total = product[:, HD:] + sum_ref[h, rows] * scale
        product = product[:, :HD] + acc_ref[h, rows] * scale
        out_ref[rows, h * HD : (h + 1) * HD] = (product / total).astype(out_ref.dtype)

    in_turn(units_of(query_ref.shape[1]), score, finish)


def attend_far(live, queries, own_keys, far, near):
    keys_here = far.shape[2] * BLK
    return pl.pallas_call(
        far_kernel,
        out_shape=jax.ShapeDtypeStruct(queries.shape, queries.dtype),
        in_specs=[SMEM] + [VMEM] * 6,
        out_specs=VMEM,
        scratch_shapes=[
            pltpu.VMEM((2 * HD, keys_here), jnp.bfloat16),
            pltpu.VMEM((keys_here, 2 * HD), jnp.bfloat16),
        ],
        compiler_params=LARGE,
    )(live, queries, own_keys, far, *near)


def own_block(keys, values, heads, head_rank):
    if heads == 2:
        columns = lambda rank: jnp.stack(
            [lax.dynamic_slice_in_dim(x, rank * HD, HD, 1) for x in (keys, values)]
        )
        mine = columns(head_rank)
        came = lax.ppermute(columns(1 - head_rank), "head", [(0, 1), (1, 0)])
        return jnp.where(
            head_rank == 0,
            jnp.concatenate([mine, came], axis=1),
            jnp.concatenate([came, mine], axis=1),
        )
    by_head = jnp.stack([keys, values]).reshape(2, -1, heads, HD).transpose(2, 0, 1, 3)
    own = lax.all_to_all(by_head, "head", split_axis=0, concat_axis=0, tiled=True)
    return own.transpose(1, 0, 2, 3).reshape(2, BLK, HD)


def on_device(heads, ranks, queries, keys, values, selected):
    lists = selected[0]
    picks = lists.shape[1] - 1
    head_rank = lax.axis_index("head")
    ctx_rank = lax.axis_index("ctx")
    share = keys.shape[0] // ranks

    spread = spread_rows(keys, values, heads, ranks)
    spread = lax.all_to_all(spread, ("head", "ctx"), split_axis=0, concat_axis=0, tiled=True)
    spread = spread.reshape(heads, ranks, 2, share, HD)
    if share % 16:
        spread = spread.transpose(1, 2, 0, 3, 4).reshape(1, ranks, 2, heads * share, HD)

    far = pick_pieces(lists, spread, ranks, picks)
    far = lax.all_to_all(far, "ctx", split_axis=0, concat_axis=0, tiled=True)
    far = far.reshape(ranks, 2, picks, -1, HD)

    own = own_block(keys, values, heads, head_rank)
    near = attend_near(queries, own[0], own[1])

    chosen = lax.dynamic_index_in_dim(lists, ctx_rank, 0, keepdims=False)[1:]
    live = (chosen != ctx_rank).astype(jnp.int32)
    return attend_far(live, queries, own[0], far, near)


def solution(mesh):
    return jax.shard_map(
        functools.partial(on_device, mesh.shape["head"], mesh.shape["ctx"]),
        mesh=mesh,
        in_specs=(
            P("ctx", "head"),
            P(("ctx", "head"), None),
            P(("ctx", "head"), None),
            P("head", None, None),
        ),
        out_specs=P("ctx", "head"),
        check_vma=False,
    )
```

```python
import functools
import math

import jax
import jax.numpy as jnp
from jax import lax
from jax.experimental import pallas as pl
from jax.experimental.pallas import tpu as pltpu
from jax.sharding import PartitionSpec as P

HD = 128
BLK = 512
CHUNK = 256
FACTOR = math.log2(math.e) / math.sqrt(HD)
SMALL = pltpu.CompilerParams(vmem_limit_bytes=2 * 1024 * 1024)
LARGE = pltpu.CompilerParams(vmem_limit_bytes=12 * 1024 * 1024)
VMEM = pl.BlockSpec(memory_space=pltpu.VMEM)
SMEM = pl.BlockSpec(memory_space=pltpu.SMEM)
ANY = pl.BlockSpec(memory_space=pl.ANY)


def spread_kernel(key_ref, value_ref, key_out, value_out, sems):
    peers = key_out.shape[0]
    ranks = key_ref.shape[0]
    copies = []
    for kv, (ref, out) in enumerate(((key_ref, key_out), (value_ref, value_out))):
        for h in range(peers // ranks):
            copies.append(
                pltpu.make_async_copy(
                    ref.at[:, :, h * HD : (h + 1) * HD],
                    out.at[h * ranks : (h + 1) * ranks],
                    sems.at[kv, h],
                )
            )
    for copy in copies:
        copy.start()
    for copy in copies:
        copy.wait()


def spread_rows(keys, values, heads, ranks):
    share = keys.shape[0] // ranks
    if share % 16 == 0:
        part = jax.ShapeDtypeStruct((heads * ranks, share, HD), keys.dtype)
        return pl.pallas_call(
            spread_kernel,
            out_shape=[part, part],
            in_specs=[ANY, ANY],
            out_specs=[ANY, ANY],
            scratch_shapes=[pltpu.SemaphoreType.DMA((2, heads))],
            compiler_params=SMALL,
        )(keys.reshape(ranks, share, heads * HD), values.reshape(ranks, share, heads * HD))
    split = lambda x: x.reshape(ranks, share, heads, HD).transpose(2, 0, 1, 3)
    return [split(x).reshape(heads * ranks, share, HD) for x in (keys, values)]


def pick_kernel(lists_ref, pieces_ref, out_ref, sem):
    receivers, picks = out_ref.shape[:2]
    for receiver in range(receivers):
        for s in range(picks):
            block = lists_ref[receiver, s + 1]
            pltpu.make_async_copy(pieces_ref.at[:, block], out_ref.at[receiver, s], sem).start()
    pltpu.make_async_copy(out_ref, out_ref, sem).wait()


def pick_pieces(lists, pieces, receivers, picks):
    parts, _, rows, _ = pieces.shape
    return pl.pallas_call(
        pick_kernel,
        out_shape=jax.ShapeDtypeStruct((receivers, picks, parts, rows, HD), pieces.dtype),
        in_specs=[SMEM, ANY],
        out_specs=ANY,
        scratch_shapes=[pltpu.SemaphoreType.DMA],
        compiler_params=SMALL,
    )(lists, pieces)


def split_queries(query_rows):
    scaled = query_rows.astype(jnp.float32) * FACTOR
    high = scaled.astype(jnp.bfloat16)
    low = (scaled - high.astype(jnp.float32)).astype(jnp.bfloat16)
    return jnp.concatenate([high, low], axis=1)


def units_of(columns):
    return [(h, begin) for h in range(columns // HD) for begin in range(0, BLK, CHUNK)]


def in_turn(units, score, finish):
    held = score(*units[0])
    for i, unit in enumerate(units):
        later = score(*units[i + 1]) if i + 1 < len(units) else None
        finish(*unit, held)
        held = later


def near_kernel(query_ref, key_ref, value_ref, top_ref, sum_ref, acc_ref, turned):
    turned[:HD] = key_ref[...].T
    turned[HD:] = turned[:HD]
    values = jnp.concatenate([value_ref[...], jnp.ones(value_ref.shape, jnp.bfloat16)], axis=1)

    def score(h, begin):
        query_rows = split_queries(query_ref[begin : begin + CHUNK, h * HD : (h + 1) * HD])
        end = begin + CHUNK
        scores = jnp.dot(query_rows, turned[:, :end], preferred_element_type=jnp.float32)
        row_ids = lax.broadcasted_iota(jnp.int32, scores.shape, 0) + begin
        col_ids = lax.broadcasted_iota(jnp.int32, scores.shape, 1)
        return jnp.where(row_ids >= col_ids, scores, -jnp.inf)

    def finish(h, begin, scores):
        rows = slice(begin, begin + CHUNK)
        top = jnp.max(scores, axis=1, keepdims=True)
        weights = jnp.exp2(scores - top).astype(jnp.bfloat16)
        product = jnp.dot(weights, values[: begin + CHUNK], preferred_element_type=jnp.float32)
        top_ref[h, rows] = jnp.broadcast_to(top, (CHUNK, HD))
        sum_ref[h, rows] = product[:, HD:]
        acc_ref[h, rows] = product[:, :HD]

    in_turn(units_of(query_ref.shape[1]), score, finish)


def attend_near(queries, own_keys, own_values):
    rows, columns = queries.shape
    part = jax.ShapeDtypeStruct((columns // HD, rows, HD), jnp.float32)
    return pl.pallas_call(
        near_kernel,
        out_shape=[part, part, part],
        in_specs=[VMEM] * 3,
        out_specs=[VMEM] * 3,
        scratch_shapes=[pltpu.VMEM((2 * HD, BLK), jnp.bfloat16)],
        compiler_params=LARGE,
        cost_estimate=pl.CostEstimate(
            flops=4 * columns * rows * BLK, bytes_accessed=4 << 20, transcendentals=0
        ),
    )(queries, own_keys, own_values)


def weigh_kernel(live_ref, query_ref, key_ref, far_ref, top_ref, weight_ref, scale_ref, turned):
    picks = far_ref.shape[1]
    spare = jnp.broadcast_to(key_ref[0:1, :], (BLK, HD))
    for s in range(picks):
        key_rows = jnp.where(live_ref[s] > 0, far_ref[:, s].reshape(BLK, HD), spare)
        turned[:HD, s * BLK : (s + 1) * BLK] = key_rows.T
    turned[HD:] = turned[:HD]

    def score(h, begin):
        query_rows = split_queries(query_ref[begin : begin + CHUNK, h * HD : (h + 1) * HD])
        return jnp.dot(query_rows, turned[...], preferred_element_type=jnp.float32)

    def finish(h, begin, scores):
        rows = slice(begin, begin + CHUNK)
        near_top = top_ref[h, rows]
        top = jnp.maximum(jnp.max(scores, axis=1, keepdims=True), near_top[:, :1])
        weight_ref[h, rows] = jnp.exp2(scores - top).astype(jnp.bfloat16)
        scale_ref[h, rows] = jnp.exp2(near_top - top)

    in_turn(units_of(query_ref.shape[1]), score, finish)


def weigh_far(live, queries, own_keys, far_keys, near_top):
    rows, columns = queries.shape
    keys_here = far_keys.shape[1] * BLK
    heads_here = columns // HD
    return pl.pallas_call(
        weigh_kernel,
        out_shape=[
            jax.ShapeDtypeStruct((heads_here, rows, keys_here), jnp.bfloat16),
            jax.ShapeDtypeStruct((heads_here, rows, HD), jnp.float32),
        ],
        in_specs=[SMEM] + [VMEM] * 4,
        out_specs=[VMEM] * 2,
        scratch_shapes=[pltpu.VMEM((2 * HD, keys_here), jnp.bfloat16)],
        compiler_params=LARGE,
        cost_estimate=pl.CostEstimate(
            flops=8 * columns * rows * keys_here, bytes_accessed=8 << 20, transcendentals=0
        ),
    )(live, queries, own_keys, far_keys, near_top)


def gather_kernel(
    live_ref, weight_ref, far_ref, scale_ref, sum_ref, acc_ref, out_ref, valued, ready, sems
):
    picks = far_ref.shape[1]
    for s in range(picks):
        rows = slice(s * BLK, (s + 1) * BLK)
        live = live_ref[s] > 0
        value_rows = far_ref[:, s].reshape(BLK, HD)
        none = jnp.zeros_like(value_rows)
        valued[rows, :HD] = jnp.where(live, value_rows, none)
        valued[rows, HD:] = jnp.where(live, jnp.ones_like(value_rows), none)
    copies = []
    for h in range(weight_ref.shape[0]):
        product = jnp.dot(weight_ref[h], valued[...], preferred_element_type=jnp.float32)
        scale = scale_ref[h]
        total = product[:, HD:] + sum_ref[h] * scale
        ready[h] = ((product[:, :HD] + acc_ref[h] * scale) / total).astype(ready.dtype)
        columns = slice(h * HD, (h + 1) * HD)
        copies.append(pltpu.make_async_copy(ready.at[h], out_ref.at[:, columns], sems.at[h]))
        copies[-1].start()
    for copy in copies:
        copy.wait()


def gather_far(live, weights, far_values, scale, near_sum, near_acc):
    heads_here, rows, keys_here = weights.shape
    return pl.pallas_call(
        gather_kernel,
        out_shape=jax.ShapeDtypeStruct((rows, heads_here * HD), jnp.bfloat16),
        in_specs=[SMEM] + [VMEM] * 5,
        out_specs=ANY,
        scratch_shapes=[
            pltpu.VMEM((keys_here, 2 * HD), jnp.bfloat16),
            pltpu.VMEM((heads_here, rows, HD), jnp.bfloat16),
            pltpu.SemaphoreType.DMA((heads_here,)),
        ],
        compiler_params=LARGE,
    )(live, weights, far_values, scale, near_sum, near_acc)


def own_block(keys, values, heads, head_rank):
    if heads == 2:
        columns = lambda rank: jnp.stack(
            [lax.dynamic_slice_in_dim(x, rank * HD, HD, 1) for x in (keys, values)]
        )
        mine = columns(head_rank)
        came = lax.ppermute(columns(1 - head_rank), "head", [(0, 1), (1, 0)])
        return jnp.where(
            head_rank == 0,
            jnp.concatenate([mine, came], axis=1),
            jnp.concatenate([came, mine], axis=1),
        )
    by_head = jnp.stack([keys, values]).reshape(2, -1, heads, HD).transpose(2, 0, 1, 3)
    own = lax.all_to_all(by_head, "head", split_axis=0, concat_axis=0, tiled=True)
    return own.transpose(1, 0, 2, 3).reshape(2, BLK, HD)


def on_device(heads, ranks, queries, keys, values, selected):
    lists = selected[0]
    picks = lists.shape[1] - 1
    head_rank = lax.axis_index("head")
    ctx_rank = lax.axis_index("ctx")
    share = keys.shape[0] // ranks

    def spread_to_ranks(part):
        part = lax.all_to_all(part, ("head", "ctx"), split_axis=0, concat_axis=0, tiled=True)
        part = part.reshape(heads, ranks, share, HD)
        if share % 16:
            part = part.transpose(1, 0, 2, 3).reshape(1, ranks, heads * share, HD)
        return part

    def send_picked(pieces):
        far = pick_pieces(lists, pieces, ranks, picks)
        far = lax.all_to_all(far, "ctx", split_axis=0, concat_axis=0, tiled=True)
        return far.reshape(ranks, picks, -1, HD)

    key_part, value_part = spread_rows(keys, values, heads, ranks)
    key_part = spread_to_ranks(key_part)
    value_part = spread_to_ranks(value_part)
    far_keys = send_picked(key_part)
    far_values = send_picked(value_part)

    own = own_block(keys, values, heads, head_rank)
    near_top, near_sum, near_acc = attend_near(queries, own[0], own[1])

    chosen = lax.dynamic_index_in_dim(lists, ctx_rank, 0, keepdims=False)[1:]
    live = (chosen != ctx_rank).astype(jnp.int32)
    weights, scale = weigh_far(live, queries, own[0], far_keys, near_top)
    return gather_far(live, weights, far_values, scale, near_sum, near_acc)


def solution(mesh):
    return jax.shard_map(
        functools.partial(on_device, mesh.shape["head"], mesh.shape["ctx"]),
        mesh=mesh,
        in_specs=(
            P("ctx", "head"),
            P(("ctx", "head"), None),
            P(("ctx", "head"), None),
            P("head", None, None),
        ),
        out_specs=P("ctx", "head"),
        check_vma=False,
    )
```

```python
import functools
import math

import jax
import jax.numpy as jnp
from jax import lax
from jax.experimental import pallas as pl
from jax.experimental.pallas import tpu as pltpu
from jax.sharding import PartitionSpec as P

HD = 128
BLK = 512
CHUNK = 128
AHEAD = 2
FACTOR = math.log2(math.e) / math.sqrt(HD)
SMALL = pltpu.CompilerParams(vmem_limit_bytes=2 * 1024 * 1024)
LARGE = pltpu.CompilerParams(vmem_limit_bytes=12 * 1024 * 1024)
VMEM = pl.BlockSpec(memory_space=pltpu.VMEM)
ANY = pl.BlockSpec(memory_space=pl.ANY)


def in_vmem(*arrays):
    return [pltpu.with_memory_space_constraint(x, pltpu.VMEM) for x in arrays]


def pack_kernel(key_ref, value_ref, out_ref, sems):
    copies = [
        pltpu.make_async_copy(ref, out_ref.at[:, kv], sems.at[kv])
        for kv, ref in enumerate((key_ref, value_ref))
    ]
    for copy in copies:
        copy.start()
    for copy in copies:
        copy.wait()


def pack_rows(keys, values, ranks):
    held, columns = keys.shape
    share = held // ranks
    keys = keys.reshape(ranks, share, columns)
    values = values.reshape(ranks, share, columns)
    if share % 16:
        return jnp.stack([keys, values], axis=1)
    return pl.pallas_call(
        pack_kernel,
        out_shape=pltpu.VMEM((ranks, 2, share, columns), keys.dtype),
        in_specs=[ANY, ANY],
        out_specs=VMEM,
        scratch_shapes=[pltpu.SemaphoreType.DMA((2,))],
        compiler_params=SMALL,
    )(*[pltpu.with_memory_space_constraint(x, pltpu.HBM) for x in (keys, values)])


def pick_kernel(lists_ref, pieces_ref, out_ref):
    heads, receivers, picks = out_ref.shape[:3]
    lists = lists_ref[...]
    for h in range(heads):
        for receiver in range(receivers):
            for s in range(picks):
                block = lists[h, receiver, s + 1]
                out_ref[h, receiver, s] = pieces_ref[block, :, :, h * HD : (h + 1) * HD]


def pick_pieces(lists, pieces):
    heads, ranks, slots = lists.shape
    share = pieces.shape[2]
    if share % 16:
        by_head = pieces.reshape(ranks, 2, share, heads, HD).transpose(3, 0, 1, 2, 4)
        return jax.vmap(lambda list_, part: part[list_[:, 1:]])(lists, by_head)
    return pl.pallas_call(
        pick_kernel,
        out_shape=pltpu.VMEM((heads, ranks, slots - 1, 2, share, HD), pieces.dtype),
        in_specs=[VMEM, VMEM],
        out_specs=VMEM,
        compiler_params=SMALL,
    )(*in_vmem(lists, pieces))


def units_of(heads_here):
    return [(h, begin) for h in range(heads_here) for begin in range(0, BLK, CHUNK)]


def in_turn(units, score, finish):
    held = [score(*unit) for unit in units[: AHEAD - 1]]
    for i, unit in enumerate(units):
        if i + AHEAD - 1 < len(units):
            held.append(score(*units[i + AHEAD - 1]))
        finish(*unit, held.pop(0))


def near_kernel(
    query_ref, key_ref, value_ref, split_ref, top_ref, sum_ref, acc_ref, turned, valued
):
    turned[:HD] = key_ref[...].T
    turned[HD:] = turned[:HD]
    valued[:, :HD] = value_ref[...]
    valued[:, HD:] = jnp.ones(value_ref.shape, valued.dtype)
    heads_here = query_ref.shape[1] // HD

    for h in range(heads_here):
        scaled = query_ref[:, h * HD : (h + 1) * HD].astype(jnp.float32) * FACTOR
        high = scaled.astype(jnp.bfloat16)
        split_ref[h, :, :HD] = high
        split_ref[h, :, HD:] = (scaled - high.astype(jnp.float32)).astype(jnp.bfloat16)

    def score(h, begin):
        end = begin + CHUNK
        scores = jnp.dot(
            split_ref[h, begin:end], turned[:, :end], preferred_element_type=jnp.float32
        )
        row_ids = lax.broadcasted_iota(jnp.int32, scores.shape, 0) + begin
        col_ids = lax.broadcasted_iota(jnp.int32, scores.shape, 1)
        return jnp.where(row_ids >= col_ids, scores, -jnp.inf)

    def finish(h, begin, scores):
        rows = slice(begin, begin + CHUNK)
        top = jnp.max(scores, axis=1, keepdims=True)
        weights = jnp.exp2(scores - top).astype(jnp.bfloat16)
        product = jnp.dot(
            weights, valued[: begin + CHUNK], preferred_element_type=jnp.float32
        )
        top_ref[h, rows] = jnp.broadcast_to(top, (CHUNK, HD))
        sum_ref[h, rows] = product[:, HD:]
        acc_ref[h, rows] = product[:, :HD]

    in_turn(units_of(heads_here), score, finish)


def attend_near(queries, own_keys, own_values):
    rows, columns = queries.shape
    heads_here = columns // HD
    part = pltpu.VMEM((heads_here, rows, HD), jnp.float32)
    return pl.pallas_call(
        near_kernel,
        out_shape=[pltpu.VMEM((heads_here, rows, 2 * HD), jnp.bfloat16), part, part, part],
        in_specs=[VMEM] * 3,
        out_specs=[VMEM] * 4,
        scratch_shapes=[
            pltpu.VMEM((2 * HD, BLK), jnp.bfloat16),
            pltpu.VMEM((BLK, 2 * HD), jnp.bfloat16),
        ],
        compiler_params=LARGE,
        cost_estimate=pl.CostEstimate(
            flops=4 * columns * rows * BLK, bytes_accessed=4 << 20, transcendentals=0
        ),
    )(queries, own_keys, own_values)


def far_kernel(
    live_ref, split_ref, key_ref, far_ref, top_ref, sum_ref, acc_ref, out_ref,
    turned, valued, ready, sems,
):
    heads_here = split_ref.shape[0]
    spare = jnp.broadcast_to(key_ref[0:1, :], (BLK, HD))
    none = jnp.zeros((BLK, HD), jnp.bfloat16)
    for s in range(far_ref.shape[1]):
        rows = slice(s * BLK, (s + 1) * BLK)
        live = jnp.broadcast_to(live_ref[s], (BLK, HD)) > 0
        turned[:HD, rows] = jnp.where(live, far_ref[:, s, 0].reshape(BLK, HD), spare).T
        valued[rows, :HD] = jnp.where(live, far_ref[:, s, 1].reshape(BLK, HD), none)
        valued[rows, HD:] = jnp.where(live, jnp.ones_like(none), none)
    turned[HD:] = turned[:HD]
    copies = []

    def score(h, begin):
        query_rows = split_ref[h, begin : begin + CHUNK]
        return jnp.dot(query_rows, turned[...], preferred_element_type=jnp.float32)

    def finish(h, begin, scores):
        rows = slice(begin, begin + CHUNK)
        near_top = top_ref[h, rows]
        top = jnp.maximum(jnp.max(scores, axis=1, keepdims=True), near_top[:, :1])
        weights = jnp.exp2(scores - top).astype(jnp.bfloat16)
        product = jnp.dot(weights, valued[...], preferred_element_type=jnp.float32)
        scale = jnp.exp2(near_top - top)
        total = product[:, HD:] + sum_ref[h, rows] * scale
        product = product[:, :HD] + acc_ref[h, rows] * scale
        ready[h, rows] = (product / total).astype(ready.dtype)
        if begin + CHUNK == BLK:
            columns = slice(h * HD, (h + 1) * HD)
            copies.append(pltpu.make_async_copy(ready.at[h], out_ref.at[:, columns], sems.at[h]))
            copies[-1].start()

    in_turn(units_of(heads_here), score, finish)
    for copy in copies:
        copy.wait()


def attend_far(live, own_keys, far, near):
    split, near_top, near_sum, near_acc = in_vmem(*near)
    heads_here, rows, _ = near_top.shape
    keys_here = far.shape[1] * BLK
    return pl.pallas_call(
        far_kernel,
        out_shape=jax.ShapeDtypeStruct((rows, heads_here * HD), jnp.bfloat16),
        in_specs=[VMEM] * 7,
        out_specs=ANY,
        scratch_shapes=[
            pltpu.VMEM((2 * HD, keys_here), jnp.bfloat16),
            pltpu.VMEM((keys_here, 2 * HD), jnp.bfloat16),
            pltpu.VMEM((heads_here, rows, HD), jnp.bfloat16),
            pltpu.SemaphoreType.DMA((heads_here,)),
        ],
        compiler_params=LARGE,
    )(*in_vmem(live), split, *in_vmem(own_keys, far), near_top, near_sum, near_acc)


def other_head(x):
    return lax.ppermute(x, "head", [(0, 1), (1, 0)])


def own_block(keys, values, heads, head_rank):
    if heads == 2:
        columns = lambda rank: jnp.stack(
            [lax.dynamic_slice_in_dim(x, rank * HD, HD, 1) for x in (keys, values)]
        )
        mine = columns(head_rank)
        came = other_head(columns(1 - head_rank))
        return jnp.where(
            head_rank == 0,
            jnp.concatenate([mine, came], axis=1),
            jnp.concatenate([came, mine], axis=1),
        )
    by_head = jnp.stack([keys, values]).reshape(2, -1, heads, HD).transpose(2, 0, 1, 3)
    own = lax.all_to_all(by_head, "head", split_axis=0, concat_axis=0, tiled=True)
    return own.transpose(1, 0, 2, 3).reshape(2, BLK, HD)


def lists_of_heads(lists, heads, head_rank):
    if heads == 2:
        came = other_head(lists)
        return jnp.where(head_rank == 0, jnp.stack([lists, came]), jnp.stack([came, lists]))
    copies = jnp.broadcast_to(lists[None], (heads, *lists.shape))
    return lax.all_to_all(copies, "head", split_axis=0, concat_axis=0, tiled=True)


def on_device(heads, ranks, queries, keys, values, selected):
    lists = selected[0]
    picks = lists.shape[1] - 1
    head_rank = lax.axis_index("head")
    ctx_rank = lax.axis_index("ctx")
    share = keys.shape[0] // ranks

    pieces = pack_rows(keys, values, ranks)
    pieces = lax.all_to_all(pieces, "ctx", split_axis=0, concat_axis=0, tiled=True)

    far = pick_pieces(lists_of_heads(lists, heads, head_rank), pieces)
    far = far.reshape(heads * ranks, picks, 2, share, HD)
    far = lax.all_to_all(far, ("head", "ctx"), split_axis=0, concat_axis=0, tiled=True)
    if share % 16:
        far = far.transpose(1, 2, 0, 3, 4).reshape(1, picks, 2, BLK, HD)

    own = own_block(keys, values, heads, head_rank)
    near = attend_near(queries, own[0], own[1])

    chosen = lax.dynamic_index_in_dim(lists, ctx_rank, 0, keepdims=False)[1:]
    live = (chosen != ctx_rank).astype(jnp.float32)
    live = jnp.broadcast_to(live[:, None, None], (picks, 1, HD))
    return attend_far(live, own[0], far, near)


def solution(mesh):
    return jax.shard_map(
        functools.partial(on_device, mesh.shape["head"], mesh.shape["ctx"]),
        mesh=mesh,
        in_specs=(
            P("ctx", "head"),
            P(("ctx", "head"), None),
            P(("ctx", "head"), None),
            P("head", None, None),
        ),
        out_specs=P("ctx", "head"),
        check_vma=False,
    )
```

```python
import functools
import math

import jax
import jax.numpy as jnp
from jax import lax
from jax.experimental import pallas as pl
from jax.experimental.pallas import tpu as pltpu
from jax.sharding import PartitionSpec as P

HD = 128
BLK = 512
CHUNK = 128
AHEAD = 2
PARTS = 4
FACTOR = math.log2(math.e) / math.sqrt(HD)
SMALL = pltpu.CompilerParams(vmem_limit_bytes=2 * 1024 * 1024)
LARGE = pltpu.CompilerParams(vmem_limit_bytes=12 * 1024 * 1024)
VMEM = pl.BlockSpec(memory_space=pltpu.VMEM)
ANY = pl.BlockSpec(memory_space=pl.ANY)


def in_vmem(*arrays):
    return [pltpu.with_memory_space_constraint(x, pltpu.VMEM) for x in arrays]


def pack_kernel(key_ref, value_ref, out_ref, held, sems):
    ranks = key_ref.shape[0]
    step = ranks // PARTS
    arrive, leave = [], []
    for part in range(PARTS):
        rows = slice(part * step, (part + 1) * step)
        for kv, ref in enumerate((key_ref, value_ref)):
            place = held.at[rows, kv]
            arrive.append(pltpu.make_async_copy(ref.at[rows], place, sems.at[0, part, kv]))
            leave.append(
                pltpu.make_async_copy(place, out_ref.at[rows, kv], sems.at[1, part, kv])
            )
    for copy in arrive:
        copy.start()
    for copy, after in zip(arrive, leave):
        copy.wait()
        after.start()
    for copy in leave:
        copy.wait()


def pack_rows(keys, values, ranks):
    held, columns = keys.shape
    share = held // ranks
    keys = keys.reshape(ranks, share, columns)
    values = values.reshape(ranks, share, columns)
    if share % 16 or ranks % PARTS:
        return jnp.stack([keys, values], axis=1)
    shape = (ranks, 2, share, columns)
    return pl.pallas_call(
        pack_kernel,
        out_shape=jax.ShapeDtypeStruct(shape, keys.dtype),
        in_specs=[ANY, ANY],
        out_specs=ANY,
        scratch_shapes=[
            pltpu.VMEM(shape, keys.dtype),
            pltpu.SemaphoreType.DMA((2, PARTS, 2)),
        ],
        compiler_params=SMALL,
    )(*[pltpu.with_memory_space_constraint(x, pltpu.HBM) for x in (keys, values)])


def pick_kernel(lists_ref, pieces_ref, out_ref):
    heads, receivers, picks = out_ref.shape[:3]
    lists = lists_ref[...]
    for h in range(heads):
        for receiver in range(receivers):
            for s in range(picks):
                block = lists[h, receiver, s + 1]
                out_ref[h, receiver, s] = pieces_ref[block, :, :, h * HD : (h + 1) * HD]


def pick_pieces(lists, pieces):
    heads, ranks, slots = lists.shape
    share = pieces.shape[2]
    if share % 16:
        by_head = pieces.reshape(ranks, 2, share, heads, HD).transpose(3, 0, 1, 2, 4)
        return jax.vmap(lambda list_, part: part[list_[:, 1:]])(lists, by_head)
    return pl.pallas_call(
        pick_kernel,
        out_shape=pltpu.VMEM((heads, ranks, slots - 1, 2, share, HD), pieces.dtype),
        in_specs=[VMEM, VMEM],
        out_specs=VMEM,
        compiler_params=SMALL,
    )(*in_vmem(lists, pieces))


def units_of(heads_here):
    return [(h, begin) for h in range(heads_here) for begin in range(0, BLK, CHUNK)]


def in_turn(units, score, finish):
    held = [score(*unit) for unit in units[: AHEAD - 1]]
    for i, unit in enumerate(units):
        if i + AHEAD - 1 < len(units):
            held.append(score(*units[i + AHEAD - 1]))
        finish(*unit, held.pop(0))


def split_queries(query_rows):
    scaled = query_rows.astype(jnp.float32) * FACTOR
    high = scaled.astype(jnp.bfloat16)
    low = (scaled - high.astype(jnp.float32)).astype(jnp.bfloat16)
    return jnp.concatenate([high, low], axis=1)


def near_kernel(
    query_ref, key_ref, value_ref, level_ref, mean_ref, turned, valued
):
    turned[:HD] = key_ref[...].T
    turned[HD:] = turned[:HD]
    valued[:, :HD] = value_ref[...]
    valued[:, HD:] = jnp.ones(value_ref.shape, valued.dtype)

    def score(h, begin):
        end = begin + CHUNK
        query_rows = split_queries(query_ref[begin:end, h * HD : (h + 1) * HD])
        scores = jnp.dot(query_rows, turned[:, :end], preferred_element_type=jnp.float32)
        row_ids = lax.broadcasted_iota(jnp.int32, scores.shape, 0) + begin
        col_ids = lax.broadcasted_iota(jnp.int32, scores.shape, 1)
        return jnp.where(row_ids >= col_ids, scores, -jnp.inf)

    def finish(h, begin, scores):
        rows = slice(begin, begin + CHUNK)
        top = jnp.max(scores, axis=1, keepdims=True)
        weights = jnp.exp2(scores - top).astype(jnp.bfloat16)
        product = jnp.dot(
            weights, valued[: begin + CHUNK], preferred_element_type=jnp.float32
        )
        level_ref[h, rows] = top + jnp.log2(product[:, HD:])
        mean_ref[h, rows] = product[:, :HD] / product[:, HD:]

    in_turn(units_of(query_ref.shape[1] // HD), score, finish)


def attend_near(queries, own_keys, own_values):
    rows, columns = queries.shape
    return pl.pallas_call(
        near_kernel,
        out_shape=[pltpu.VMEM((columns // HD, rows, HD), jnp.float32)] * 2,
        in_specs=[VMEM] * 3,
        out_specs=[VMEM] * 2,
        scratch_shapes=[
            pltpu.VMEM((2 * HD, BLK), jnp.bfloat16),
            pltpu.VMEM((BLK, 2 * HD), jnp.bfloat16),
        ],
        compiler_params=LARGE,
        cost_estimate=pl.CostEstimate(
            flops=4 * columns * rows * BLK, bytes_accessed=4 << 20, transcendentals=0
        ),
    )(queries, own_keys, own_values)


def far_kernel(
    live_ref, query_ref, key_ref, far_ref, level_ref, mean_ref, out_ref, turned, valued, ready, sems
):
    spare = jnp.broadcast_to(key_ref[...], (BLK, HD))
    none = jnp.zeros((BLK, HD), jnp.bfloat16)
    for s in range(far_ref.shape[1]):
        rows = slice(s * BLK, (s + 1) * BLK)
        live = jnp.broadcast_to(live_ref[s], (BLK, HD)) > 0
        turned[:HD, rows] = jnp.where(live, far_ref[:, s, 0].reshape(BLK, HD), spare).T
        valued[rows, :HD] = jnp.where(live, far_ref[:, s, 1].reshape(BLK, HD), none)
        valued[rows, HD:] = jnp.where(live, jnp.ones_like(none), none)
    turned[HD:] = turned[:HD]
    copies = []

    def score(h, begin):
        query_rows = split_queries(query_ref[begin : begin + CHUNK, h * HD : (h + 1) * HD])
        return jnp.dot(query_rows, turned[...], preferred_element_type=jnp.float32)

    def finish(h, begin, scores):
        rows = slice(begin, begin + CHUNK)
        level = level_ref[h, rows]
        top = jnp.maximum(jnp.max(scores, axis=1, keepdims=True), level[:, :1])
        weights = jnp.exp2(scores - top).astype(jnp.bfloat16)
        product = jnp.dot(weights, valued[...], preferred_element_type=jnp.float32)
        scale = jnp.exp2(level - top)
        total = product[:, HD:] + scale
        product = product[:, :HD] + mean_ref[h, rows] * scale
        ready[h, rows] = (product / total).astype(ready.dtype)
        if begin + CHUNK == BLK:
            columns = slice(h * HD, (h + 1) * HD)
            copies.append(pltpu.make_async_copy(ready.at[h], out_ref.at[:, columns], sems.at[h]))
            copies[-1].start()

    in_turn(units_of(query_ref.shape[1] // HD), score, finish)
    for copy in copies:
        copy.wait()


def attend_far(live, queries, first_key, far, near):
    rows, columns = queries.shape
    keys_here = far.shape[1] * BLK
    return pl.pallas_call(
        far_kernel,
        out_shape=jax.ShapeDtypeStruct(queries.shape, queries.dtype),
        in_specs=[VMEM] * 6,
        out_specs=ANY,
        scratch_shapes=[
            pltpu.VMEM((2 * HD, keys_here), jnp.bfloat16),
            pltpu.VMEM((keys_here, 2 * HD), jnp.bfloat16),
            pltpu.VMEM((columns // HD, rows, HD), jnp.bfloat16),
            pltpu.SemaphoreType.DMA((columns // HD,)),
        ],
        compiler_params=LARGE,
    )(*in_vmem(live, queries, first_key, far, *near))


def other_head(x):
    return lax.ppermute(x, "head", [(0, 1), (1, 0)])


def own_block(keys, values, heads, head_rank):
    if heads == 2:
        columns = lambda rank: jnp.stack(
            [lax.dynamic_slice_in_dim(x, rank * HD, HD, 1) for x in (keys, values)]
        )
        mine = columns(head_rank)
        came = other_head(columns(1 - head_rank))
        return jnp.where(
            head_rank == 0,
            jnp.concatenate([mine, came], axis=1),
            jnp.concatenate([came, mine], axis=1),
        )
    by_head = jnp.stack([keys, values]).reshape(2, -1, heads, HD).transpose(2, 0, 1, 3)
    own = lax.all_to_all(by_head, "head", split_axis=0, concat_axis=0, tiled=True)
    return own.transpose(1, 0, 2, 3).reshape(2, BLK, HD)


def lists_of_heads(lists, heads, head_rank):
    if heads == 2:
        came = other_head(lists)
        return jnp.where(head_rank == 0, jnp.stack([lists, came]), jnp.stack([came, lists]))
    copies = jnp.broadcast_to(lists[None], (heads, *lists.shape))
    return lax.all_to_all(copies, "head", split_axis=0, concat_axis=0, tiled=True)


def on_device(heads, ranks, queries, keys, values, selected):
    lists = selected[0]
    picks = lists.shape[1] - 1
    head_rank = lax.axis_index("head")
    ctx_rank = lax.axis_index("ctx")
    share = keys.shape[0] // ranks

    pieces = pack_rows(keys, values, ranks)
    pieces = lax.all_to_all(pieces, "ctx", split_axis=0, concat_axis=0, tiled=True)

    own = own_block(keys, values, heads, head_rank)
    every_list = lists_of_heads(lists, heads, head_rank)
    pieces, own, every_list = lax.optimization_barrier((pieces, own, every_list))

    far = pick_pieces(every_list, pieces)
    far = far.reshape(heads * ranks, picks, 2, share, HD)
    far = lax.all_to_all(far, ("head", "ctx"), split_axis=0, concat_axis=0, tiled=True)
    if share % 16:
        far = far.transpose(1, 2, 0, 3, 4).reshape(1, picks, 2, BLK, HD)

    near = attend_near(queries, own[0], own[1])

    chosen = lax.dynamic_index_in_dim(lists, ctx_rank, 0, keepdims=False)[1:]
    live = (chosen != ctx_rank).astype(jnp.float32)
    live = jnp.broadcast_to(live[:, None, None], (picks, 1, HD))
    return attend_far(live, queries, own[0, :1], far, near)


def solution(mesh):
    return jax.shard_map(
        functools.partial(on_device, mesh.shape["head"], mesh.shape["ctx"]),
        mesh=mesh,
        in_specs=(
            P("ctx", "head"),
            P(("ctx", "head"), None),
            P(("ctx", "head"), None),
            P("head", None, None),
        ),
        out_specs=P("ctx", "head"),
        check_vma=False,
    )
```

```python
import functools
import itertools
import math

import jax
import jax.numpy as jnp
from jax import lax
from jax.experimental import pallas as pl
from jax.experimental.pallas import tpu as pltpu
from jax.sharding import PartitionSpec as P

HD = 128
BLK = 512
CHUNK = 128
AHEAD = 2
PARTS = 4
FACTOR = math.log2(math.e) / math.sqrt(HD)
SMALL = pltpu.CompilerParams(vmem_limit_bytes=2 * 1024 * 1024)
LARGE = pltpu.CompilerParams(vmem_limit_bytes=12 * 1024 * 1024)
VMEM = pl.BlockSpec(memory_space=pltpu.VMEM)
ANY = pl.BlockSpec(memory_space=pl.ANY)


def in_vmem(*arrays):
    return [pltpu.with_memory_space_constraint(x, pltpu.VMEM) for x in arrays]


def pack_kernel(key_ref, value_ref, out_ref, held, sems):
    ranks = key_ref.shape[0]
    step = ranks // PARTS
    arrive, leave = [], []
    for part in range(PARTS):
        rows = slice(part * step, (part + 1) * step)
        for kv, ref in enumerate((key_ref, value_ref)):
            place = held.at[rows, kv]
            arrive.append(pltpu.make_async_copy(ref.at[rows], place, sems.at[0, part, kv]))
            leave.append(
                pltpu.make_async_copy(place, out_ref.at[rows, kv], sems.at[1, part, kv])
            )
    for copy in arrive:
        copy.start()
    for copy, after in zip(arrive, leave):
        copy.wait()
        after.start()
    for copy in leave:
        copy.wait()


def pack_rows(keys, values, ranks):
    held, columns = keys.shape
    share = held // ranks
    keys = keys.reshape(ranks, share, columns)
    values = values.reshape(ranks, share, columns)
    if share % 16 or ranks % PARTS:
        return jnp.stack([keys, values], axis=1)
    shape = (ranks, 2, share, columns)
    return pl.pallas_call(
        pack_kernel,
        out_shape=jax.ShapeDtypeStruct(shape, keys.dtype),
        in_specs=[ANY, ANY],
        out_specs=ANY,
        scratch_shapes=[
            pltpu.VMEM(shape, keys.dtype),
            pltpu.SemaphoreType.DMA((2, PARTS, 2)),
        ],
        compiler_params=SMALL,
    )(*[pltpu.with_memory_space_constraint(x, pltpu.HBM) for x in (keys, values)])


def pick_kernel(lists_ref, pieces_ref, out_ref):
    heads, receivers, picks = out_ref.shape[:3]
    lists = lists_ref[...]
    for h in range(heads):
        for receiver in range(receivers):
            for s in range(picks):
                block = lists[h, receiver, s + 1]
                out_ref[h, receiver, s] = pieces_ref[block, :, :, h * HD : (h + 1) * HD]


def pick_pieces(lists, pieces):
    heads, ranks, slots = lists.shape
    share = pieces.shape[2]
    if share % 16:
        by_head = pieces.reshape(ranks, 2, share, heads, HD).transpose(3, 0, 1, 2, 4)
        return jax.vmap(lambda list_, part: part[list_[:, 1:]])(lists, by_head)
    return pl.pallas_call(
        pick_kernel,
        out_shape=pltpu.VMEM((heads, ranks, slots - 1, 2, share, HD), pieces.dtype),
        in_specs=[VMEM, VMEM],
        out_specs=VMEM,
        compiler_params=SMALL,
    )(*in_vmem(lists, pieces))


def units_of(heads_here):
    return [(h, begin) for h in range(heads_here) for begin in range(0, BLK, CHUNK)]


def in_turn(units, score, finish):
    held = [score(*unit) for unit in units[: AHEAD - 1]]
    for i, unit in enumerate(units):
        if i + AHEAD - 1 < len(units):
            held.append(score(*units[i + AHEAD - 1]))
        finish(*unit, held.pop(0))


def split_queries(query_rows):
    scaled = query_rows.astype(jnp.float32) * FACTOR
    high = scaled.astype(jnp.bfloat16)
    low = (scaled - high.astype(jnp.float32)).astype(jnp.bfloat16)
    return jnp.concatenate([high, low], axis=1)


def near_kernel(
    query_ref, key_ref, value_ref, level_ref, mean_ref, turned, valued
):
    turned[:HD] = key_ref[...].T
    turned[HD:] = turned[:HD]
    valued[:, :HD] = value_ref[...]
    valued[:, HD:] = jnp.ones(value_ref.shape, valued.dtype)

    def score(h, begin):
        end = begin + CHUNK
        query_rows = split_queries(query_ref[begin:end, h * HD : (h + 1) * HD])
        scores = jnp.dot(query_rows, turned[:, :end], preferred_element_type=jnp.float32)
        row_ids = lax.broadcasted_iota(jnp.int32, scores.shape, 0) + begin
        col_ids = lax.broadcasted_iota(jnp.int32, scores.shape, 1)
        return jnp.where(row_ids >= col_ids, scores, -jnp.inf)

    def finish(h, begin, scores):
        rows = slice(begin, begin + CHUNK)
        top = jnp.max(scores, axis=1, keepdims=True)
        weights = jnp.exp2(scores - top).astype(jnp.bfloat16)
        product = jnp.dot(
            weights, valued[: begin + CHUNK], preferred_element_type=jnp.float32
        )
        level_ref[h, rows] = top + jnp.log2(product[:, HD:])
        mean_ref[h, rows] = product[:, :HD] / product[:, HD:]

    in_turn(units_of(query_ref.shape[1] // HD), score, finish)


def attend_near(queries, own_keys, own_values):
    rows, columns = queries.shape
    return pl.pallas_call(
        near_kernel,
        out_shape=[pltpu.VMEM((columns // HD, rows, HD), jnp.float32)] * 2,
        in_specs=[VMEM] * 3,
        out_specs=[VMEM] * 2,
        scratch_shapes=[
            pltpu.VMEM((2 * HD, BLK), jnp.bfloat16),
            pltpu.VMEM((BLK, 2 * HD), jnp.bfloat16),
        ],
        compiler_params=LARGE,
        cost_estimate=pl.CostEstimate(
            flops=4 * columns * rows * BLK, bytes_accessed=4 << 20, transcendentals=0
        ),
    )(queries, own_keys, own_values)


def far_kernel(
    live_ref, query_ref, far_ref, level_ref, mean_ref, out_ref, turned, valued, ready, sems
):
    heads_here = query_ref.shape[1] // HD
    picks = far_ref.shape[1]

    def leave(h):
        columns = slice(h * HD, (h + 1) * HD)
        return pltpu.make_async_copy(ready.at[h], out_ref.at[:, columns], sems.at[h])

    def attend(slots):
        keys_here = len(slots) * BLK
        for place, s in enumerate(slots):
            rows = slice(place * BLK, (place + 1) * BLK)
            turned[:HD, rows] = far_ref[:, s, 0].reshape(BLK, HD).T
            valued[rows, :HD] = far_ref[:, s, 1].reshape(BLK, HD)
        turned[HD:, :keys_here] = turned[:HD, :keys_here]
        valued[:keys_here, HD:] = jnp.ones((keys_here, HD), valued.dtype)

        def score(h, begin):
            query_rows = split_queries(query_ref[begin : begin + CHUNK, h * HD : (h + 1) * HD])
            return jnp.dot(
                query_rows, turned[:, :keys_here], preferred_element_type=jnp.float32
            )

        def finish(h, begin, scores):
            rows = slice(begin, begin + CHUNK)
            level = level_ref[h, rows]
            top = jnp.maximum(jnp.max(scores, axis=1, keepdims=True), level[:, :1])
            weights = jnp.exp2(scores - top).astype(jnp.bfloat16)
            product = jnp.dot(weights, valued[:keys_here], preferred_element_type=jnp.float32)
            scale = jnp.exp2(level - top)
            total = product[:, HD:] + scale
            product = product[:, :HD] + mean_ref[h, rows] * scale
            ready[h, rows] = (product / total).astype(ready.dtype)
            if begin + CHUNK == BLK:
                leave(h).start()

        in_turn(units_of(heads_here), score, finish)

    flags = live_ref[...]
    live = [flags[0, s] > 0 for s in range(picks)]
    for which in itertools.product((False, True), repeat=picks):
        slots = [s for s in range(picks) if which[s]]
        met = functools.reduce(
            jnp.logical_and, [flag if on else ~flag for flag, on in zip(live, which)]
        )

        @pl.when(met)
        def _():
            if slots:
                attend(slots)
            else:
                for h in range(heads_here):
                    ready[h] = mean_ref[h].astype(ready.dtype)
                    leave(h).start()

    for h in range(heads_here):
        leave(h).wait()


def attend_far(live, queries, far, near):
    rows, columns = queries.shape
    keys_here = far.shape[1] * BLK
    return pl.pallas_call(
        far_kernel,
        out_shape=jax.ShapeDtypeStruct(queries.shape, queries.dtype),
        in_specs=[VMEM] * 5,
        out_specs=ANY,
        scratch_shapes=[
            pltpu.VMEM((2 * HD, keys_here), jnp.bfloat16),
            pltpu.VMEM((keys_here, 2 * HD), jnp.bfloat16),
            pltpu.VMEM((columns // HD, rows, HD), jnp.bfloat16),
            pltpu.SemaphoreType.DMA((columns // HD,)),
        ],
        compiler_params=LARGE,
    )(*in_vmem(live, queries, far, *near))


def other_head(x):
    return lax.ppermute(x, "head", [(0, 1), (1, 0)])


def own_block(keys, values, heads, head_rank):
    if heads == 2:
        columns = lambda rank: jnp.stack(
            [lax.dynamic_slice_in_dim(x, rank * HD, HD, 1) for x in (keys, values)]
        )
        mine = columns(head_rank)
        came = other_head(columns(1 - head_rank))
        return jnp.where(
            head_rank == 0,
            jnp.concatenate([mine, came], axis=1),
            jnp.concatenate([came, mine], axis=1),
        )
    by_head = jnp.stack([keys, values]).reshape(2, -1, heads, HD).transpose(2, 0, 1, 3)
    own = lax.all_to_all(by_head, "head", split_axis=0, concat_axis=0, tiled=True)
    return own.transpose(1, 0, 2, 3).reshape(2, BLK, HD)


def lists_of_heads(lists, heads, head_rank):
    if heads == 2:
        came = other_head(lists)
        return jnp.where(head_rank == 0, jnp.stack([lists, came]), jnp.stack([came, lists]))
    copies = jnp.broadcast_to(lists[None], (heads, *lists.shape))
    return lax.all_to_all(copies, "head", split_axis=0, concat_axis=0, tiled=True)


def on_device(heads, ranks, queries, keys, values, selected):
    lists = selected[0]
    picks = lists.shape[1] - 1
    head_rank = lax.axis_index("head")
    ctx_rank = lax.axis_index("ctx")
    share = keys.shape[0] // ranks

    pieces = pack_rows(keys, values, ranks)
    pieces = lax.all_to_all(pieces, "ctx", split_axis=0, concat_axis=0, tiled=True)

    own = own_block(keys, values, heads, head_rank)
    every_list = lists_of_heads(lists, heads, head_rank)
    pieces, own, every_list = lax.optimization_barrier((pieces, own, every_list))

    far = pick_pieces(every_list, pieces)
    far = far.reshape(heads * ranks, picks, 2, share, HD)
    far = lax.all_to_all(far, ("head", "ctx"), split_axis=0, concat_axis=0, tiled=True)
    if share % 16:
        far = far.transpose(1, 2, 0, 3, 4).reshape(1, picks, 2, BLK, HD)

    near = attend_near(queries, own[0], own[1])

    chosen = lax.dynamic_index_in_dim(lists, ctx_rank, 0, keepdims=False)[1:]
    live = (chosen != ctx_rank).astype(jnp.int32)[None]
    return attend_far(live, queries, far, near)


def solution(mesh):
    return jax.shard_map(
        functools.partial(on_device, mesh.shape["head"], mesh.shape["ctx"]),
        mesh=mesh,
        in_specs=(
            P("ctx", "head"),
            P(("ctx", "head"), None),
            P(("ctx", "head"), None),
            P("head", None, None),
        ),
        out_specs=P("ctx", "head"),
        check_vma=False,
    )
```

```python
import functools
import itertools
import math

import jax
import jax.numpy as jnp
from jax import lax
from jax.experimental import pallas as pl
from jax.experimental.pallas import tpu as pltpu
from jax.sharding import PartitionSpec as P

HD = 128
BLK = 512
CHUNK = 128
AHEAD = 2
PARTS = 4
FACTOR = math.log2(math.e) / math.sqrt(HD)
SMALL = pltpu.CompilerParams(vmem_limit_bytes=2 * 1024 * 1024)
LARGE = pltpu.CompilerParams(vmem_limit_bytes=12 * 1024 * 1024)
VMEM = pl.BlockSpec(memory_space=pltpu.VMEM)
ANY = pl.BlockSpec(memory_space=pl.ANY)


def in_vmem(*arrays):
    return [pltpu.with_memory_space_constraint(x, pltpu.VMEM) for x in arrays]


def pack_kernel(key_ref, value_ref, out_ref, held, sems):
    ranks = key_ref.shape[0]
    step = ranks // PARTS
    arrive, leave = [], []
    for part in range(PARTS):
        rows = slice(part * step, (part + 1) * step)
        for kv, ref in enumerate((key_ref, value_ref)):
            place = held.at[rows, kv]
            arrive.append(pltpu.make_async_copy(ref.at[rows], place, sems.at[0, part, kv]))
            leave.append(
                pltpu.make_async_copy(place, out_ref.at[rows, kv], sems.at[1, part, kv])
            )
    for copy in arrive:
        copy.start()
    for copy, after in zip(arrive, leave):
        copy.wait()
        after.start()
    for copy in leave:
        copy.wait()


def pack_rows(keys, values, ranks):
    held, columns = keys.shape
    share = held // ranks
    keys = keys.reshape(ranks, share, columns)
    values = values.reshape(ranks, share, columns)
    if share % 16 or ranks % PARTS:
        return jnp.stack([keys, values], axis=1)
    shape = (ranks, 2, share, columns)
    return pl.pallas_call(
        pack_kernel,
        out_shape=jax.ShapeDtypeStruct(shape, keys.dtype),
        in_specs=[ANY, ANY],
        out_specs=ANY,
        scratch_shapes=[
            pltpu.VMEM(shape, keys.dtype),
            pltpu.SemaphoreType.DMA((2, PARTS, 2)),
        ],
        compiler_params=SMALL,
    )(*[pltpu.with_memory_space_constraint(x, pltpu.HBM) for x in (keys, values)])


def pick_kernel(lists_ref, pieces_ref, out_ref):
    heads, receivers, picks = out_ref.shape[:3]
    lists = lists_ref[...]
    for h in range(heads):
        for receiver in range(receivers):
            for s in range(picks):
                block = lists[h, receiver, s + 1]
                out_ref[h, receiver, s] = pieces_ref[block, :, :, h * HD : (h + 1) * HD]


def pick_pieces(lists, pieces):
    heads, ranks, slots = lists.shape
    share = pieces.shape[2]
    if share % 16:
        by_head = pieces.reshape(ranks, 2, share, heads, HD).transpose(3, 0, 1, 2, 4)
        return jax.vmap(lambda list_, part: part[list_[:, 1:]])(lists, by_head)
    return pl.pallas_call(
        pick_kernel,
        out_shape=pltpu.VMEM((heads, ranks, slots - 1, 2, share, HD), pieces.dtype),
        in_specs=[VMEM, VMEM],
        out_specs=VMEM,
        compiler_params=SMALL,
    )(*in_vmem(lists, pieces))


def units_of(heads_here, size):
    return [(h, begin, begin + size) for h in range(heads_here) for begin in range(0, BLK, size)]


def in_turn(units, score, finish):
    held = [score(*unit) for unit in units[: AHEAD - 1]]
    for i, unit in enumerate(units):
        if i + AHEAD - 1 < len(units):
            held.append(score(*units[i + AHEAD - 1]))
        finish(*unit, held.pop(0))


def split_queries(query_rows):
    scaled = query_rows.astype(jnp.float32) * FACTOR
    high = scaled.astype(jnp.bfloat16)
    low = (scaled - high.astype(jnp.float32)).astype(jnp.bfloat16)
    return jnp.concatenate([high, low], axis=1)


def near_kernel(
    query_ref, key_ref, value_ref, level_ref, mean_ref, turned, valued
):
    turned[:HD] = key_ref[...].T
    turned[HD:] = turned[:HD]
    valued[:, :HD] = value_ref[...]
    valued[:, HD:] = jnp.ones(value_ref.shape, valued.dtype)

    def score(h, begin, end):
        query_rows = split_queries(query_ref[begin:end, h * HD : (h + 1) * HD])
        scores = jnp.dot(query_rows, turned[:, :end], preferred_element_type=jnp.float32)
        row_ids = lax.broadcasted_iota(jnp.int32, scores.shape, 0) + begin
        col_ids = lax.broadcasted_iota(jnp.int32, scores.shape, 1)
        return jnp.where(row_ids >= col_ids, scores, -jnp.inf)

    def finish(h, begin, end, scores):
        rows = slice(begin, end)
        top = jnp.max(scores, axis=1, keepdims=True)
        weights = jnp.exp2(scores - top).astype(jnp.bfloat16)
        product = jnp.dot(weights, valued[:end], preferred_element_type=jnp.float32)
        level_ref[h, rows] = top + jnp.log2(product[:, HD:])
        mean_ref[h, rows] = product[:, :HD] / product[:, HD:]

    in_turn(units_of(query_ref.shape[1] // HD, CHUNK), score, finish)


def attend_near(queries, own_keys, own_values):
    rows, columns = queries.shape
    return pl.pallas_call(
        near_kernel,
        out_shape=[pltpu.VMEM((columns // HD, rows, HD), jnp.float32)] * 2,
        in_specs=[VMEM] * 3,
        out_specs=[VMEM] * 2,
        scratch_shapes=[
            pltpu.VMEM((2 * HD, BLK), jnp.bfloat16),
            pltpu.VMEM((BLK, 2 * HD), jnp.bfloat16),
        ],
        compiler_params=LARGE,
        cost_estimate=pl.CostEstimate(
            flops=4 * columns * rows * BLK, bytes_accessed=4 << 20, transcendentals=0
        ),
    )(queries, own_keys, own_values)


def far_kernel(
    live_ref, query_ref, far_ref, level_ref, mean_ref, out_ref, turned, valued, ready, sems
):
    heads_here = query_ref.shape[1] // HD
    picks = far_ref.shape[1]

    def leave(h):
        columns = slice(h * HD, (h + 1) * HD)
        return pltpu.make_async_copy(ready.at[h], out_ref.at[:, columns], sems.at[h])

    def attend(slots):
        keys_here = len(slots) * BLK
        for place, s in enumerate(slots):
            rows = slice(place * BLK, (place + 1) * BLK)
            turned[:HD, rows] = far_ref[:, s, 0].reshape(BLK, HD).T
            valued[rows, :HD] = far_ref[:, s, 1].reshape(BLK, HD)
        turned[HD:, :keys_here] = turned[:HD, :keys_here]
        valued[:keys_here, HD:] = jnp.ones((keys_here, HD), valued.dtype)

        def score(h, begin, end):
            query_rows = split_queries(query_ref[begin:end, h * HD : (h + 1) * HD])
            return jnp.dot(
                query_rows, turned[:, :keys_here], preferred_element_type=jnp.float32
            )

        def finish(h, begin, end, scores):
            rows = slice(begin, end)
            level = level_ref[h, rows]
            top = jnp.maximum(jnp.max(scores, axis=1, keepdims=True), level[:, :1])
            weights = jnp.exp2(scores - top).astype(jnp.bfloat16)
            product = jnp.dot(weights, valued[:keys_here], preferred_element_type=jnp.float32)
            scale = jnp.exp2(level - top)
            total = product[:, HD:] + scale
            product = product[:, :HD] + mean_ref[h, rows] * scale
            ready[h, rows] = (product / total).astype(ready.dtype)
            if end == BLK:
                leave(h).start()

        size = CHUNK if len(slots) == picks else 2 * CHUNK
        in_turn(units_of(heads_here, size), score, finish)

    flags = live_ref[...]
    live = [flags[0, s] > 0 for s in range(picks)]
    for which in itertools.product((False, True), repeat=picks):
        slots = [s for s in range(picks) if which[s]]
        met = functools.reduce(
            jnp.logical_and, [flag if on else ~flag for flag, on in zip(live, which)]
        )

        @pl.when(met)
        def _():
            if slots:
                attend(slots)
            else:
                for h in range(heads_here):
                    ready[h] = mean_ref[h].astype(ready.dtype)
                    leave(h).start()

    for h in range(heads_here):
        leave(h).wait()


def attend_far(live, queries, far, near):
    rows, columns = queries.shape
    keys_here = far.shape[1] * BLK
    return pl.pallas_call(
        far_kernel,
        out_shape=jax.ShapeDtypeStruct(queries.shape, queries.dtype),
        in_specs=[VMEM] * 5,
        out_specs=ANY,
        scratch_shapes=[
            pltpu.VMEM((2 * HD, keys_here), jnp.bfloat16),
            pltpu.VMEM((keys_here, 2 * HD), jnp.bfloat16),
            pltpu.VMEM((columns // HD, rows, HD), jnp.bfloat16),
            pltpu.SemaphoreType.DMA((columns // HD,)),
        ],
        compiler_params=LARGE,
    )(*in_vmem(live, queries, far, *near))


def other_head(x):
    return lax.ppermute(x, "head", [(0, 1), (1, 0)])


def own_block(keys, values, heads, head_rank):
    if heads == 2:
        columns = lambda rank: jnp.stack(
            [lax.dynamic_slice_in_dim(x, rank * HD, HD, 1) for x in (keys, values)]
        )
        mine = columns(head_rank)
        came = other_head(columns(1 - head_rank))
        return jnp.where(
            head_rank == 0,
            jnp.concatenate([mine, came], axis=1),
            jnp.concatenate([came, mine], axis=1),
        )
    by_head = jnp.stack([keys, values]).reshape(2, -1, heads, HD).transpose(2, 0, 1, 3)
    own = lax.all_to_all(by_head, "head", split_axis=0, concat_axis=0, tiled=True)
    return own.transpose(1, 0, 2, 3).reshape(2, BLK, HD)


def lists_of_heads(lists, heads, head_rank):
    if heads == 2:
        came = other_head(lists)
        return jnp.where(head_rank == 0, jnp.stack([lists, came]), jnp.stack([came, lists]))
    copies = jnp.broadcast_to(lists[None], (heads, *lists.shape))
    return lax.all_to_all(copies, "head", split_axis=0, concat_axis=0, tiled=True)


def on_device(heads, ranks, queries, keys, values, selected):
    lists = selected[0]
    picks = lists.shape[1] - 1
    head_rank = lax.axis_index("head")
    ctx_rank = lax.axis_index("ctx")
    share = keys.shape[0] // ranks

    pieces = pack_rows(keys, values, ranks)
    backwards = [list(range(ranks))[::-1]]
    pieces = lax.all_to_all(
        pieces, "ctx", split_axis=0, concat_axis=0, axis_index_groups=backwards, tiled=True
    )

    own = own_block(keys, values, heads, head_rank)
    every_list = ranks - 1 - lists_of_heads(lists, heads, head_rank)
    pieces, own, every_list = lax.optimization_barrier((pieces, own, every_list))

    far = pick_pieces(every_list, pieces)
    far = far.reshape(heads * ranks, picks, 2, share, HD)
    far = lax.all_to_all(far, ("head", "ctx"), split_axis=0, concat_axis=0, tiled=True)
    if share % 16:
        far = far.transpose(1, 2, 0, 3, 4).reshape(1, picks, 2, BLK, HD)

    near = attend_near(queries, own[0], own[1])

    chosen = lax.dynamic_index_in_dim(lists, ctx_rank, 0, keepdims=False)[1:]
    live = (chosen != ctx_rank).astype(jnp.int32)[None]
    return attend_far(live, queries, far, near)


def solution(mesh):
    return jax.shard_map(
        functools.partial(on_device, mesh.shape["head"], mesh.shape["ctx"]),
        mesh=mesh,
        in_specs=(
            P("ctx", "head"),
            P(("ctx", "head"), None),
            P(("ctx", "head"), None),
            P("head", None, None),
        ),
        out_specs=P("ctx", "head"),
        check_vma=False,
    )
```

```python
import functools
import itertools
import math

import jax
import jax.numpy as jnp
from jax import lax
from jax.experimental import pallas as pl
from jax.experimental.pallas import tpu as pltpu
from jax.sharding import PartitionSpec as P

HD = 128
BLK = 512
CHUNK = 128
AHEAD = 2
FACTOR = math.log2(math.e) / math.sqrt(HD)
SMALL = pltpu.CompilerParams(vmem_limit_bytes=2 * 1024 * 1024)
LARGE = pltpu.CompilerParams(vmem_limit_bytes=12 * 1024 * 1024)
VMEM = pl.BlockSpec(memory_space=pltpu.VMEM)
ANY = pl.BlockSpec(memory_space=pl.ANY)


def in_vmem(*arrays):
    return [pltpu.with_memory_space_constraint(x, pltpu.VMEM) for x in arrays]


def pack_kernel(key_ref, value_ref, slots_ref, out_ref, slots_out, sems, slots_sem):
    heads = out_ref.shape[0]
    copies = [
        pltpu.make_async_copy(
            ref.at[:, :, h * HD : (h + 1) * HD], out_ref.at[h, :, kv], sems.at[kv, h]
        )
        for kv, ref in enumerate((key_ref, value_ref))
        for h in range(heads)
    ]
    copies.append(pltpu.make_async_copy(slots_ref, slots_out, slots_sem))
    for copy in copies:
        copy.start()
    for copy in copies:
        copy.wait()


def pack(keys, values, slots, heads, ranks):
    rows, columns = keys.shape
    share = rows // ranks
    if share % 16:
        both = jnp.stack([keys, values]).reshape(2, ranks, share, heads, HD)
        return both.transpose(3, 1, 0, 2, 4), slots
    operands = [keys.reshape(ranks, share, columns), values.reshape(ranks, share, columns), slots]
    return pl.pallas_call(
        pack_kernel,
        out_shape=[
            pltpu.VMEM((heads, ranks, 2, share, HD), keys.dtype),
            pltpu.VMEM(slots.shape, slots.dtype),
        ],
        in_specs=[ANY] * 3,
        out_specs=[VMEM] * 2,
        scratch_shapes=[pltpu.SemaphoreType.DMA((2, heads)), pltpu.SemaphoreType.DMA],
        compiler_params=SMALL,
    )(*[pltpu.with_memory_space_constraint(x, pltpu.HBM) for x in operands])


def pick_kernel(order, slots_ref, pieces_ref, out_ref):
    _, picks, parts = out_ref.shape[:3]
    slots = slots_ref[...]
    for place, receiver in enumerate(order):
        for s in range(picks):
            block = slots[s + 1, 0, receiver]
            for part in range(parts):
                out_ref[place, s, part] = pieces_ref[part, block]


def pick_pieces(slots, pieces, order):
    heads, ranks, _, share, _ = pieces.shape
    if share % 16:
        return pieces.swapaxes(0, 1)[slots[1:, 0].T[jnp.array(order)]]
    return pl.pallas_call(
        functools.partial(pick_kernel, order),
        out_shape=pltpu.VMEM((ranks, slots.shape[0] - 1, heads, 2, share, HD), pieces.dtype),
        in_specs=[VMEM, VMEM],
        out_specs=VMEM,
        compiler_params=SMALL,
    )(*in_vmem(slots, pieces))


def units_of(heads_here, size):
    return [(h, begin, begin + size) for h in range(heads_here) for begin in range(0, BLK, size)]


def in_turn(units, score, finish):
    held = [score(*unit) for unit in units[: AHEAD - 1]]
    for i, unit in enumerate(units):
        if i + AHEAD - 1 < len(units):
            held.append(score(*units[i + AHEAD - 1]))
        finish(*unit, held.pop(0))


def split_queries(query_rows):
    scaled = query_rows.astype(jnp.float32) * FACTOR
    high = scaled.astype(jnp.bfloat16)
    low = (scaled - high.astype(jnp.float32)).astype(jnp.bfloat16)
    return jnp.concatenate([high, low], axis=1)


def near_kernel(
    query_ref, key_ref, value_ref, level_ref, mean_ref, turned, valued
):
    turned[:HD] = key_ref[...].T
    turned[HD:] = turned[:HD]
    valued[:, :HD] = value_ref[...]
    valued[:, HD:] = jnp.ones(value_ref.shape, valued.dtype)

    def score(h, begin, end):
        query_rows = split_queries(query_ref[begin:end, h * HD : (h + 1) * HD])
        scores = jnp.dot(query_rows, turned[:, :end], preferred_element_type=jnp.float32)
        row_ids = lax.broadcasted_iota(jnp.int32, scores.shape, 0) + begin
        col_ids = lax.broadcasted_iota(jnp.int32, scores.shape, 1)
        return jnp.where(row_ids >= col_ids, scores, -jnp.inf)

    def finish(h, begin, end, scores):
        rows = slice(begin, end)
        top = jnp.max(scores, axis=1, keepdims=True)
        weights = jnp.exp2(scores - top).astype(jnp.bfloat16)
        product = jnp.dot(weights, valued[:end], preferred_element_type=jnp.float32)
        level_ref[h, rows] = top + jnp.log2(product[:, HD:])
        mean_ref[h, rows] = product[:, :HD] / product[:, HD:]

    in_turn(units_of(query_ref.shape[1] // HD, CHUNK), score, finish)


def attend_near(queries, own_keys, own_values):
    rows, columns = queries.shape
    return pl.pallas_call(
        near_kernel,
        out_shape=[pltpu.VMEM((columns // HD, rows, HD), jnp.float32)] * 2,
        in_specs=[VMEM] * 3,
        out_specs=[VMEM] * 2,
        scratch_shapes=[
            pltpu.VMEM((2 * HD, BLK), jnp.bfloat16),
            pltpu.VMEM((BLK, 2 * HD), jnp.bfloat16),
        ],
        compiler_params=LARGE,
        cost_estimate=pl.CostEstimate(
            flops=4 * columns * rows * BLK, bytes_accessed=4 << 20, transcendentals=0
        ),
    )(*in_vmem(queries, own_keys, own_values))


def far_kernel(
    live_ref, query_ref, far_ref, level_ref, mean_ref, out_ref, turned, valued, ready, sems
):
    heads_here = query_ref.shape[1] // HD
    picks = far_ref.shape[1]

    def leave(h):
        columns = slice(h * HD, (h + 1) * HD)
        return pltpu.make_async_copy(ready.at[h], out_ref.at[:, columns], sems.at[h])

    for s in range(picks):
        place = slice(s * BLK, (s + 1) * BLK)
        turned[:HD, place] = far_ref[:, s, :, 0].reshape(BLK, HD).T
        valued[place, :HD] = far_ref[:, s, :, 1].reshape(BLK, HD)
    turned[HD:] = turned[:HD]
    valued[:, HD:] = jnp.ones((picks * BLK, HD), valued.dtype)

    def attend(first, last):
        place = slice(first * BLK, (last + 1) * BLK)

        def score(h, begin, end):
            query_rows = split_queries(query_ref[begin:end, h * HD : (h + 1) * HD])
            return jnp.dot(query_rows, turned[:, place], preferred_element_type=jnp.float32)

        def finish(h, begin, end, scores):
            rows = slice(begin, end)
            level = level_ref[h, rows]
            top = jnp.maximum(jnp.max(scores, axis=1, keepdims=True), level[:, :1])
            weights = jnp.exp2(scores - top).astype(jnp.bfloat16)
            product = jnp.dot(weights, valued[place], preferred_element_type=jnp.float32)
            scale = jnp.exp2(level - top)
            total = product[:, HD:] + scale
            product = product[:, :HD] + mean_ref[h, rows] * scale
            ready[h, rows] = (product / total).astype(ready.dtype)
            if end == BLK:
                leave(h).start()

        size = CHUNK if last > first else 2 * CHUNK
        in_turn(units_of(heads_here, size), score, finish)

    rank = lax.axis_index("ctx")

    @pl.when(rank >= picks)
    def _():
        attend(0, picks - 1)

    @pl.when(rank < picks)
    def _():
        flags = live_ref[...]
        live = [flags[0, s] > 0 for s in range(picks)]
        for which in itertools.product((False, True), repeat=picks):
            slots = [s for s in range(picks) if which[s]]
            met = functools.reduce(
                jnp.logical_and, [flag if on else ~flag for flag, on in zip(live, which)]
            )
            if len(slots) == picks:
                continue

            @pl.when(met)
            def _():
                if slots:
                    attend(slots[0], slots[-1])
                else:
                    for h in range(heads_here):
                        ready[h] = mean_ref[h].astype(ready.dtype)
                        leave(h).start()

    for h in range(heads_here):
        leave(h).wait()


def attend_far(live, queries, far, near):
    rows, columns = queries.shape
    keys_here = far.shape[1] * BLK
    return pl.pallas_call(
        far_kernel,
        out_shape=jax.ShapeDtypeStruct(queries.shape, queries.dtype),
        in_specs=[VMEM] * 5,
        out_specs=ANY,
        scratch_shapes=[
            pltpu.VMEM((2 * HD, keys_here), jnp.bfloat16),
            pltpu.VMEM((keys_here, 2 * HD), jnp.bfloat16),
            pltpu.VMEM((columns // HD, rows, HD), jnp.bfloat16),
            pltpu.SemaphoreType.DMA((columns // HD,)),
        ],
        compiler_params=LARGE,
    )(*in_vmem(live, queries, far, *near))


def other_head(x):
    return lax.ppermute(x, "head", [(0, 1), (1, 0)])


def own_block(keys, values, heads, head_rank):
    if heads == 2:
        columns = lambda rank: jnp.stack(
            [lax.dynamic_slice_in_dim(x, rank * HD, HD, 1) for x in (keys, values)]
        )
        mine = columns(head_rank)
        came = lax.ppermute(columns(1 - head_rank), "head", [(0, 1), (1, 0)])
        return jnp.where(
            head_rank == 0,
            jnp.concatenate([mine, came], axis=1),
            jnp.concatenate([came, mine], axis=1),
        )
    by_head = jnp.stack([keys, values]).reshape(2, -1, heads, HD).transpose(2, 0, 1, 3)
    own = lax.all_to_all(by_head, "head", split_axis=0, concat_axis=0, tiled=True)
    return own.transpose(1, 0, 2, 3).reshape(2, BLK, HD)


def on_device(heads, ranks, queries, keys, values, selected):
    lists = selected[0]
    picks = lists.shape[1] - 1
    head_rank = lax.axis_index("head")
    ctx_rank = lax.axis_index("ctx")
    share = keys.shape[0] // ranks

    order = [(i + ranks // 2) % ranks for i in range(ranks)]

    pieces, slots = pack(keys, values, selected.transpose(2, 0, 1), heads, ranks)
    pieces = pieces.reshape(heads * ranks, 2, share, HD)
    pieces = lax.all_to_all(pieces, ("head", "ctx"), split_axis=0, concat_axis=0, tiled=True)
    pieces = pieces.reshape(heads, ranks, 2, share, HD)

    pieces, queries, keys, values = lax.optimization_barrier((pieces, queries, keys, values))

    far = pick_pieces(slots, pieces, order)
    far = lax.all_to_all(
        far, "ctx", split_axis=0, concat_axis=0, axis_index_groups=[order], tiled=True
    )
    if share % 16:
        far = far.transpose(1, 3, 0, 2, 4, 5).reshape(1, picks, 2, BLK, HD)[:, :, None]

    own = own_block(keys, values, heads, head_rank)
    near = attend_near(queries, own[0], own[1])
    chosen = lax.dynamic_index_in_dim(lists, ctx_rank, 0, keepdims=False)[1:]
    live = (chosen != ctx_rank).astype(jnp.int32)[None]
    return attend_far(live, queries, far, near)


def solution(mesh):
    return jax.shard_map(
        functools.partial(on_device, mesh.shape["head"], mesh.shape["ctx"]),
        mesh=mesh,
        in_specs=(
            P("ctx", "head"),
            P(("ctx", "head"), None),
            P(("ctx", "head"), None),
            P("head", None, None),
        ),
        out_specs=P("ctx", "head"),
        check_vma=False,
    )
```

```python
import functools
import itertools
import math

import jax
import jax.numpy as jnp
from jax import lax
from jax.experimental import pallas as pl
from jax.experimental.pallas import tpu as pltpu
from jax.sharding import PartitionSpec as P

HD = 128
BLK = 512
CHUNK = 128
AHEAD = 2
FACTOR = math.log2(math.e) / math.sqrt(HD)
SMALL = pltpu.CompilerParams(vmem_limit_bytes=2 * 1024 * 1024)
LARGE = pltpu.CompilerParams(vmem_limit_bytes=12 * 1024 * 1024)
VMEM = pl.BlockSpec(memory_space=pltpu.VMEM)
ANY = pl.BlockSpec(memory_space=pl.ANY)


def in_vmem(*arrays):
    return [pltpu.with_memory_space_constraint(x, pltpu.VMEM) for x in arrays]


def pack_kernel(key_ref, value_ref, slots_ref, out_ref, slots_out, sems, slots_sem):
    group = lax.rem(lax.axis_index("head") + lax.axis_index("ctx"), 2)
    copies = [pltpu.make_async_copy(slots_ref, slots_out, slots_sem)]
    for turn in range(2):
        head = lax.rem(group + 1 - turn, 2)
        columns = pl.ds(pl.multiple_of(head * HD, HD), HD)
        for kv, ref in enumerate((key_ref, value_ref)):
            copies.append(
                pltpu.make_async_copy(
                    ref.at[:, :, columns], out_ref.at[:, turn, kv], sems.at[kv, turn]
                )
            )
    for copy in copies:
        copy.start()
    for copy in copies:
        copy.wait()


def pack(keys, values, slots, ranks):
    rows, columns = keys.shape
    pairs = ranks // 2
    operands = [x.reshape(pairs, rows // pairs, columns) for x in (keys, values)] + [slots]
    return pl.pallas_call(
        pack_kernel,
        out_shape=[
            pltpu.VMEM((pairs, 2, 2, rows // pairs, HD), keys.dtype),
            pltpu.VMEM(slots.shape, slots.dtype),
        ],
        in_specs=[ANY] * 3,
        out_specs=[VMEM] * 2,
        scratch_shapes=[pltpu.SemaphoreType.DMA((2, 2)), pltpu.SemaphoreType.DMA],
        compiler_params=SMALL,
    )(*[pltpu.with_memory_space_constraint(x, pltpu.HBM) for x in operands])


def pick_kernel(order, slots_ref, pieces_ref, out_ref):
    ranks, picks = out_ref.shape[:2]
    slots = slots_ref[...]
    for place, receiver in enumerate(order):
        for s in range(picks):
            out_ref[place, s] = pieces_ref[ranks - 1 - slots[s + 1, 0, receiver]]


def pick_pieces(slots, pieces, order):
    ranks, *rest = pieces.shape
    return pl.pallas_call(
        functools.partial(pick_kernel, order),
        out_shape=pltpu.VMEM((ranks, slots.shape[0] - 1, *rest), pieces.dtype),
        in_specs=[VMEM, VMEM],
        out_specs=VMEM,
        compiler_params=SMALL,
    )(*in_vmem(slots, pieces))


def send_selected(keys, values, slots, ranks, order):
    pieces, slots = pack(keys, values, slots, ranks)
    pieces = pieces.reshape(ranks, *pieces.shape[2:])
    groups = [
        [((g + r) % 2) * ranks + r for r in reversed(range(ranks))] for g in range(2)
    ]
    pieces = lax.all_to_all(
        pieces,
        ("head", "ctx"),
        split_axis=0,
        concat_axis=0,
        axis_index_groups=groups,
        tiled=True,
    )
    return pieces, slots


def send_selected_of_many(keys, values, heads, ranks):
    share = keys.shape[0] // ranks
    pieces = jnp.stack([keys, values]).reshape(2, ranks, share, heads, HD)
    pieces = pieces.transpose(3, 1, 0, 2, 4).reshape(heads * ranks, 2, share, HD)
    pieces = lax.all_to_all(pieces, ("head", "ctx"), split_axis=0, concat_axis=0, tiled=True)
    pieces = pieces.reshape(heads, ranks, 2, share, HD)
    return pieces.transpose(1, 2, 0, 3, 4).reshape(ranks, 2, heads * share, HD)


def units_of(heads_here, size):
    return [(h, begin, begin + size) for h in range(heads_here) for begin in range(0, BLK, size)]


def in_turn(units, score, finish):
    held = [score(*unit) for unit in units[: AHEAD - 1]]
    for i, unit in enumerate(units):
        if i + AHEAD - 1 < len(units):
            held.append(score(*units[i + AHEAD - 1]))
        finish(*unit, held.pop(0))


def split_queries(query_rows):
    scaled = query_rows.astype(jnp.float32) * FACTOR
    high = scaled.astype(jnp.bfloat16)
    low = (scaled - high.astype(jnp.float32)).astype(jnp.bfloat16)
    return jnp.concatenate([high, low], axis=1)


def near_kernel(
    query_ref, key_ref, value_ref, level_ref, mean_ref, turned, valued
):
    turned[:HD] = key_ref[...].T
    turned[HD:] = turned[:HD]
    valued[:, :HD] = value_ref[...]
    valued[:, HD:] = jnp.ones(value_ref.shape, valued.dtype)

    def score(h, begin, end):
        query_rows = split_queries(query_ref[begin:end, h * HD : (h + 1) * HD])
        scores = jnp.dot(query_rows, turned[:, :end], preferred_element_type=jnp.float32)
        row_ids = lax.broadcasted_iota(jnp.int32, scores.shape, 0) + begin
        col_ids = lax.broadcasted_iota(jnp.int32, scores.shape, 1)
        return jnp.where(row_ids >= col_ids, scores, -jnp.inf)

    def finish(h, begin, end, scores):
        rows = slice(begin, end)
        top = jnp.max(scores, axis=1, keepdims=True)
        weights = jnp.exp2(scores - top).astype(jnp.bfloat16)
        product = jnp.dot(weights, valued[:end], preferred_element_type=jnp.float32)
        level_ref[h, rows] = top + jnp.log2(product[:, HD:])
        mean_ref[h, rows] = product[:, :HD] / product[:, HD:]

    in_turn(units_of(query_ref.shape[1] // HD, CHUNK), score, finish)


def attend_near(queries, own_keys, own_values):
    rows, columns = queries.shape
    return pl.pallas_call(
        near_kernel,
        out_shape=[pltpu.VMEM((columns // HD, rows, HD), jnp.float32)] * 2,
        in_specs=[VMEM] * 3,
        out_specs=[VMEM] * 2,
        scratch_shapes=[
            pltpu.VMEM((2 * HD, BLK), jnp.bfloat16),
            pltpu.VMEM((BLK, 2 * HD), jnp.bfloat16),
        ],
        compiler_params=LARGE,
        cost_estimate=pl.CostEstimate(
            flops=4 * columns * rows * BLK, bytes_accessed=4 << 20, transcendentals=0
        ),
    )(*in_vmem(queries, own_keys, own_values))


def far_kernel(
    live_ref, query_ref, far_ref, level_ref, mean_ref, out_ref, turned, valued, ready, sems
):
    heads_here = query_ref.shape[1] // HD
    picks = far_ref.shape[1]

    def leave(h):
        columns = slice(h * HD, (h + 1) * HD)
        return pltpu.make_async_copy(ready.at[h], out_ref.at[:, columns], sems.at[h])

    for s in range(picks):
        place = slice(s * BLK, (s + 1) * BLK)
        turned[:HD, place] = far_ref[:, s, 0].reshape(BLK, HD).T
        valued[place, :HD] = far_ref[:, s, 1].reshape(BLK, HD)
    turned[HD:] = turned[:HD]
    valued[:, HD:] = jnp.ones((picks * BLK, HD), valued.dtype)

    def attend(first, last):
        place = slice(first * BLK, (last + 1) * BLK)

        def score(h, begin, end):
            query_rows = split_queries(query_ref[begin:end, h * HD : (h + 1) * HD])
            return jnp.dot(query_rows, turned[:, place], preferred_element_type=jnp.float32)

        def finish(h, begin, end, scores):
            rows = slice(begin, end)
            level = level_ref[h, rows]
            top = jnp.maximum(
                jnp.broadcast_to(jnp.max(scores, axis=1, keepdims=True), level.shape), level
            )
            tiles = [scores[:, i : i + HD] for i in range(0, scores.shape[1], HD)]
            weights = jnp.concatenate(
                [jnp.exp2(tile - top).astype(jnp.bfloat16) for tile in tiles], axis=1
            )
            product = jnp.dot(weights, valued[place], preferred_element_type=jnp.float32)
            scale = jnp.exp2(level - top)
            total = product[:, HD:] + scale
            product = product[:, :HD] + mean_ref[h, rows] * scale
            ready[h, rows] = (product / total).astype(ready.dtype)
            if end == BLK:
                leave(h).start()

        size = CHUNK if last > first else 2 * CHUNK
        in_turn(units_of(heads_here, size), score, finish)

    rank = lax.axis_index("ctx")

    @pl.when(rank >= picks)
    def _():
        attend(0, picks - 1)

    @pl.when(rank < picks)
    def _():
        flags = live_ref[...]
        live = [flags[0, s] > 0 for s in range(picks)]
        for which in itertools.product((False, True), repeat=picks):
            slots = [s for s in range(picks) if which[s]]
            met = functools.reduce(
                jnp.logical_and, [flag if on else ~flag for flag, on in zip(live, which)]
            )
            if len(slots) == picks:
                continue

            @pl.when(met)
            def _():
                if slots:
                    attend(slots[0], slots[-1])
                else:
                    for h in range(heads_here):
                        ready[h] = mean_ref[h].astype(ready.dtype)
                        leave(h).start()

    for h in range(heads_here):
        leave(h).wait()


def attend_far(live, queries, far, near):
    rows, columns = queries.shape
    keys_here = far.shape[1] * BLK
    return pl.pallas_call(
        far_kernel,
        out_shape=jax.ShapeDtypeStruct(queries.shape, queries.dtype),
        in_specs=[VMEM] * 5,
        out_specs=ANY,
        scratch_shapes=[
            pltpu.VMEM((2 * HD, keys_here), jnp.bfloat16),
            pltpu.VMEM((keys_here, 2 * HD), jnp.bfloat16),
            pltpu.VMEM((columns // HD, rows, HD), jnp.bfloat16),
            pltpu.SemaphoreType.DMA((columns // HD,)),
        ],
        compiler_params=LARGE,
    )(*in_vmem(live, queries, far, *near))


def other_head(x):
    return lax.ppermute(x, "head", [(0, 1), (1, 0)])


def own_block(keys, values, heads, head_rank):
    if heads == 2:
        columns = lambda rank: jnp.stack(
            [lax.dynamic_slice_in_dim(x, rank * HD, HD, 1) for x in (keys, values)]
        )
        mine = columns(head_rank)
        came = lax.ppermute(columns(1 - head_rank), "head", [(0, 1), (1, 0)])
        return jnp.where(
            head_rank == 0,
            jnp.concatenate([mine, came], axis=1),
            jnp.concatenate([came, mine], axis=1),
        )
    by_head = jnp.stack([keys, values]).reshape(2, -1, heads, HD).transpose(2, 0, 1, 3)
    own = lax.all_to_all(by_head, "head", split_axis=0, concat_axis=0, tiled=True)
    return own.transpose(1, 0, 2, 3).reshape(2, BLK, HD)


def on_device(heads, ranks, queries, keys, values, selected):
    lists = selected[0]
    picks = lists.shape[1] - 1
    head_rank = lax.axis_index("head")
    ctx_rank = lax.axis_index("ctx")
    share = keys.shape[0] // ranks

    order = [(i + ranks // 2) % ranks for i in range(ranks)]

    slots = selected.transpose(2, 0, 1)
    plain = heads == 2 and share % 8 == 0 and ranks % 2 == 0
    if plain:
        pieces, slots = send_selected(keys, values, slots, ranks, order)
    else:
        pieces = send_selected_of_many(keys, values, heads, ranks)

    pieces, queries, keys, values = lax.optimization_barrier((pieces, queries, keys, values))

    if plain:
        far = pick_pieces(slots, pieces, order)
    else:
        far = pieces[slots[1:, 0].T[jnp.array(order)]]
    far = lax.all_to_all(
        far, "ctx", split_axis=0, concat_axis=0, axis_index_groups=[order], tiled=True
    )
    if not plain:
        far = far.transpose(1, 2, 0, 3, 4).reshape(1, picks, 2, BLK, HD)

    own = own_block(keys, values, heads, head_rank)
    near = attend_near(queries, own[0], own[1])
    chosen = lax.dynamic_index_in_dim(lists, ctx_rank, 0, keepdims=False)[1:]
    live = (chosen != ctx_rank).astype(jnp.int32)[None]
    return attend_far(live, queries, far, near)


def solution(mesh):
    return jax.shard_map(
        functools.partial(on_device, mesh.shape["head"], mesh.shape["ctx"]),
        mesh=mesh,
        in_specs=(
            P("ctx", "head"),
            P(("ctx", "head"), None),
            P(("ctx", "head"), None),
            P("head", None, None),
        ),
        out_specs=P("ctx", "head"),
        check_vma=False,
    )
```

```python
import functools
import itertools
import math

import jax
import jax.numpy as jnp
from jax import lax
from jax.experimental import pallas as pl
from jax.experimental.pallas import tpu as pltpu
from jax.sharding import PartitionSpec as P

HD = 128
BLK = 512
CHUNK = 128
AHEAD = 2
FACTOR = math.log2(math.e) / math.sqrt(HD)
SMALL = pltpu.CompilerParams(vmem_limit_bytes=2 * 1024 * 1024)
LARGE = pltpu.CompilerParams(vmem_limit_bytes=12 * 1024 * 1024)
VMEM = pl.BlockSpec(memory_space=pltpu.VMEM)
ANY = pl.BlockSpec(memory_space=pl.ANY)


def in_vmem(*arrays):
    return [pltpu.with_memory_space_constraint(x, pltpu.VMEM) for x in arrays]


def pack_kernel(key_ref, value_ref, slots_ref, out_ref, slots_out, sems, slots_sem):
    group = lax.rem(lax.axis_index("head") + lax.axis_index("ctx"), 2)
    copies = [pltpu.make_async_copy(slots_ref, slots_out, slots_sem)]
    half = key_ref.shape[0] // 2
    for turn in range(2):
        head = lax.rem(group + 1 - turn, 2)
        columns = pl.ds(pl.multiple_of(head * HD, HD), HD)
        for kv, ref in enumerate((key_ref, value_ref)):
            for part in range(2):
                some = slice(part * half, (part + 1) * half)
                copies.append(
                    pltpu.make_async_copy(
                        ref.at[some, :, columns], out_ref.at[some, turn, kv], sems.at[kv, turn, part]
                    )
                )
    for copy in copies:
        copy.start()
    for copy in copies:
        copy.wait()


def pack(keys, values, slots, ranks):
    rows, columns = keys.shape
    pairs = ranks // 2
    operands = [x.reshape(pairs, rows // pairs, columns) for x in (keys, values)] + [slots]
    return pl.pallas_call(
        pack_kernel,
        out_shape=[
            pltpu.VMEM((pairs, 2, 2, rows // pairs, HD), keys.dtype),
            pltpu.VMEM(slots.shape, slots.dtype),
        ],
        in_specs=[ANY] * 3,
        out_specs=[VMEM] * 2,
        scratch_shapes=[pltpu.SemaphoreType.DMA((2, 2, 2)), pltpu.SemaphoreType.DMA],
        compiler_params=SMALL,
    )(*[pltpu.with_memory_space_constraint(x, pltpu.HBM) for x in operands])


def pick_kernel(order, slots_ref, pieces_ref, out_ref, sem):
    ranks, picks = out_ref.shape[:2]
    slots = slots_ref[...]
    for place, receiver in enumerate(order):
        for s in range(picks):
            piece = pieces_ref.at[ranks - 1 - slots[s + 1, 0, receiver]]
            pltpu.make_async_copy(piece, out_ref.at[place, s], sem).start()
    pltpu.make_async_copy(out_ref, out_ref, sem).wait()


def pick_pieces(slots, pieces, order):
    ranks, *rest = pieces.shape
    return pl.pallas_call(
        functools.partial(pick_kernel, order),
        out_shape=jax.ShapeDtypeStruct((ranks, slots.shape[0] - 1, *rest), pieces.dtype),
        in_specs=[VMEM, VMEM],
        out_specs=ANY,
        scratch_shapes=[pltpu.SemaphoreType.DMA],
        compiler_params=SMALL,
    )(*in_vmem(slots, pieces))


def send_selected(keys, values, slots, ranks, order):
    pieces, slots = pack(keys, values, slots, ranks)
    pieces = pieces.reshape(ranks, *pieces.shape[2:])
    groups = [
        [((g + r) % 2) * ranks + r for r in reversed(range(ranks))] for g in range(2)
    ]
    pieces = lax.all_to_all(
        pieces,
        ("head", "ctx"),
        split_axis=0,
        concat_axis=0,
        axis_index_groups=groups,
        tiled=True,
    )
    return pieces, slots


def send_selected_of_many(keys, values, heads, ranks):
    share = keys.shape[0] // ranks
    pieces = jnp.stack([keys, values]).reshape(2, ranks, share, heads, HD)
    pieces = pieces.transpose(3, 1, 0, 2, 4).reshape(heads * ranks, 2, share, HD)
    pieces = lax.all_to_all(pieces, ("head", "ctx"), split_axis=0, concat_axis=0, tiled=True)
    pieces = pieces.reshape(heads, ranks, 2, share, HD)
    return pieces.transpose(1, 2, 0, 3, 4).reshape(ranks, 2, heads * share, HD)


def units_of(heads_here, size):
    return [(h, begin, begin + size) for h in range(heads_here) for begin in range(0, BLK, size)]


def in_turn(units, score, finish):
    held = [score(*unit) for unit in units[: AHEAD - 1]]
    for i, unit in enumerate(units):
        if i + AHEAD - 1 < len(units):
            held.append(score(*units[i + AHEAD - 1]))
        finish(*unit, held.pop(0))


def near_kernel(
    query_ref, key_ref, value_ref, level_ref, mean_ref, turned, valued
):
    turned[...] = key_ref[...].T
    valued[:, :HD] = value_ref[...]
    valued[:, HD:] = jnp.ones(value_ref.shape, valued.dtype)

    def score(h, begin, end):
        query_rows = query_ref[begin:end, h * HD : (h + 1) * HD]
        scores = jnp.dot(query_rows, turned[:, :end], preferred_element_type=jnp.float32)
        row_ids = lax.broadcasted_iota(jnp.int32, scores.shape, 0) + begin
        col_ids = lax.broadcasted_iota(jnp.int32, scores.shape, 1)
        return jnp.where(row_ids >= col_ids, scores, -jnp.inf)

    def finish(h, begin, end, scores):
        rows = slice(begin, end)
        top = jnp.max(scores, axis=1, keepdims=True)
        weights = jnp.exp2((scores - top) * FACTOR).astype(jnp.bfloat16)
        product = jnp.dot(weights, valued[:end], preferred_element_type=jnp.float32)
        level_ref[h, rows] = top + jnp.log2(product[:, HD:]) / FACTOR
        mean_ref[h, rows] = product[:, :HD] / product[:, HD:]

    in_turn(units_of(query_ref.shape[1] // HD, CHUNK), score, finish)


def attend_near(queries, own_keys, own_values):
    rows, columns = queries.shape
    return pl.pallas_call(
        near_kernel,
        out_shape=[pltpu.VMEM((columns // HD, rows, HD), jnp.float32)] * 2,
        in_specs=[VMEM] * 3,
        out_specs=[VMEM] * 2,
        scratch_shapes=[
            pltpu.VMEM((HD, BLK), jnp.bfloat16),
            pltpu.VMEM((BLK, 2 * HD), jnp.bfloat16),
        ],
        compiler_params=LARGE,
        cost_estimate=pl.CostEstimate(
            flops=4 * columns * rows * BLK, bytes_accessed=4 << 20, transcendentals=0
        ),
    )(*in_vmem(queries, own_keys, own_values))


def far_kernel(
    live_ref, query_ref, far_ref, level_ref, mean_ref, out_ref, turned, valued, ready, sems
):
    heads_here = query_ref.shape[1] // HD
    picks = far_ref.shape[1]

    def leave(h):
        columns = slice(h * HD, (h + 1) * HD)
        return pltpu.make_async_copy(ready.at[h], out_ref.at[:, columns], sems.at[h])

    for s in range(picks):
        place = slice(s * BLK, (s + 1) * BLK)
        turned[:, place] = far_ref[:, s, 0].reshape(BLK, HD).T
        valued[place, :HD] = far_ref[:, s, 1].reshape(BLK, HD)
    valued[:, HD:] = jnp.ones((picks * BLK, HD), valued.dtype)

    def attend(first, last):
        place = slice(first * BLK, (last + 1) * BLK)

        def score(h, begin, end):
            query_rows = query_ref[begin:end, h * HD : (h + 1) * HD]
            return jnp.dot(query_rows, turned[:, place], preferred_element_type=jnp.float32)

        def finish(h, begin, end, scores):
            rows = slice(begin, end)
            level = level_ref[h, rows]
            top = jnp.maximum(
                jnp.broadcast_to(jnp.max(scores, axis=1, keepdims=True), level.shape), level
            )
            tiles = [scores[:, i : i + HD] for i in range(0, scores.shape[1], HD)]
            weights = jnp.concatenate(
                [jnp.exp2((tile - top) * FACTOR).astype(jnp.bfloat16) for tile in tiles], axis=1
            )
            product = jnp.dot(weights, valued[place], preferred_element_type=jnp.float32)
            scale = jnp.exp2((level - top) * FACTOR)
            total = product[:, HD:] + scale
            product = product[:, :HD] + mean_ref[h, rows] * scale
            ready[h, rows] = (product / total).astype(ready.dtype)
            if end == BLK:
                leave(h).start()

        in_turn(units_of(heads_here, 2 * CHUNK), score, finish)

    rank = lax.axis_index("ctx")

    @pl.when(rank >= picks)
    def _():
        attend(0, picks - 1)

    @pl.when(rank < picks)
    def _():
        flags = live_ref[...]
        live = [flags[0, s] > 0 for s in range(picks)]
        for which in itertools.product((False, True), repeat=picks):
            slots = [s for s in range(picks) if which[s]]
            met = functools.reduce(
                jnp.logical_and, [flag if on else ~flag for flag, on in zip(live, which)]
            )
            if len(slots) == picks:
                continue

            @pl.when(met)
            def _():
                if slots:
                    attend(slots[0], slots[-1])
                else:
                    for h in range(heads_here):
                        ready[h] = mean_ref[h].astype(ready.dtype)
                        leave(h).start()

    for h in range(heads_here):
        leave(h).wait()


def attend_far(live, queries, far, near):
    rows, columns = queries.shape
    keys_here = far.shape[1] * BLK
    return pl.pallas_call(
        far_kernel,
        out_shape=jax.ShapeDtypeStruct(queries.shape, queries.dtype),
        in_specs=[VMEM] * 5,
        out_specs=ANY,
        scratch_shapes=[
            pltpu.VMEM((HD, keys_here), jnp.bfloat16),
            pltpu.VMEM((keys_here, 2 * HD), jnp.bfloat16),
            pltpu.VMEM((columns // HD, rows, HD), jnp.bfloat16),
            pltpu.SemaphoreType.DMA((columns // HD,)),
        ],
        compiler_params=LARGE,
    )(*in_vmem(live, queries, far, *near))


def other_head(x):
    return lax.ppermute(x, "head", [(0, 1), (1, 0)])


def own_block(keys, values, heads, head_rank):
    if heads == 2:
        columns = lambda rank: jnp.stack(
            [lax.dynamic_slice_in_dim(x, rank * HD, HD, 1) for x in (keys, values)]
        )
        mine = columns(head_rank)
        came = lax.ppermute(columns(1 - head_rank), "head", [(0, 1), (1, 0)])
        return jnp.where(
            head_rank == 0,
            jnp.concatenate([mine, came], axis=1),
            jnp.concatenate([came, mine], axis=1),
        )
    by_head = jnp.stack([keys, values]).reshape(2, -1, heads, HD).transpose(2, 0, 1, 3)
    own = lax.all_to_all(by_head, "head", split_axis=0, concat_axis=0, tiled=True)
    return own.transpose(1, 0, 2, 3).reshape(2, BLK, HD)


def on_device(heads, ranks, queries, keys, values, selected):
    lists = selected[0]
    picks = lists.shape[1] - 1
    head_rank = lax.axis_index("head")
    ctx_rank = lax.axis_index("ctx")
    share = keys.shape[0] // ranks

    order = [(i + ranks // 2) % ranks for i in range(ranks)]

    slots = selected.transpose(2, 0, 1)
    plain = heads == 2 and share % 8 == 0 and ranks % 2 == 0
    if plain:
        pieces, slots = send_selected(keys, values, slots, ranks, order)
    else:
        pieces = send_selected_of_many(keys, values, heads, ranks)

    pieces, queries, keys, values = lax.optimization_barrier((pieces, queries, keys, values))

    if plain:
        far = pick_pieces(slots, pieces, order)
    else:
        far = pieces[slots[1:, 0].T[jnp.array(order)]]
    far = lax.all_to_all(
        far, "ctx", split_axis=0, concat_axis=0, axis_index_groups=[order], tiled=True
    )
    if not plain:
        far = far.transpose(1, 2, 0, 3, 4).reshape(1, picks, 2, BLK, HD)

    own = own_block(keys, values, heads, head_rank)
    near = attend_near(queries, own[0], own[1])
    chosen = lax.dynamic_index_in_dim(lists, ctx_rank, 0, keepdims=False)[1:]
    live = (chosen != ctx_rank).astype(jnp.int32)[None]
    return attend_far(live, queries, far, near)


def solution(mesh):
    return jax.shard_map(
        functools.partial(on_device, mesh.shape["head"], mesh.shape["ctx"]),
        mesh=mesh,
        in_specs=(
            P("ctx", "head"),
            P(("ctx", "head"), None),
            P(("ctx", "head"), None),
            P("head", None, None),
        ),
        out_specs=P("ctx", "head"),
        check_vma=False,
    )
```

```python
import functools
import math

import jax
import jax.numpy as jnp
from jax import lax
from jax.experimental import pallas as pl
from jax.experimental.pallas import tpu as pltpu
from jax.sharding import PartitionSpec as P

HD = 128
BLK = 512
CHUNK = 128
AHEAD = 2
FACTOR = math.log2(math.e) / math.sqrt(HD)
SMALL = pltpu.CompilerParams(vmem_limit_bytes=2 * 1024 * 1024)
LARGE = pltpu.CompilerParams(vmem_limit_bytes=12 * 1024 * 1024)
VMEM = pl.BlockSpec(memory_space=pltpu.VMEM)
ANY = pl.BlockSpec(memory_space=pl.ANY)


def in_vmem(*arrays):
    return [pltpu.with_memory_space_constraint(x, pltpu.VMEM) for x in arrays]


def pack_kernel(key_ref, value_ref, slots_ref, out_ref, slots_out, sems, slots_sem):
    group = lax.rem(lax.axis_index("head") + lax.axis_index("ctx"), 2)
    copies = [pltpu.make_async_copy(slots_ref, slots_out, slots_sem)]
    half = key_ref.shape[0] // 2
    for turn in range(2):
        head = lax.rem(group + 1 - turn, 2)
        columns = pl.ds(pl.multiple_of(head * HD, HD), HD)
        for kv, ref in enumerate((key_ref, value_ref)):
            for part in range(2):
                some = slice(part * half, (part + 1) * half)
                copies.append(
                    pltpu.make_async_copy(
                        ref.at[some, :, columns], out_ref.at[some, turn, kv], sems.at[kv, turn, part]
                    )
                )
    for copy in copies:
        copy.start()
    for copy in copies:
        copy.wait()


def pack(keys, values, slots, ranks):
    rows, columns = keys.shape
    pairs = ranks // 2
    operands = [x.reshape(pairs, rows // pairs, columns) for x in (keys, values)] + [slots]
    return pl.pallas_call(
        pack_kernel,
        out_shape=[
            pltpu.VMEM((pairs, 2, 2, rows // pairs, HD), keys.dtype),
            pltpu.VMEM(slots.shape, slots.dtype),
        ],
        in_specs=[ANY] * 3,
        out_specs=[VMEM] * 2,
        scratch_shapes=[pltpu.SemaphoreType.DMA((2, 2, 2)), pltpu.SemaphoreType.DMA],
        compiler_params=SMALL,
    )(*[pltpu.with_memory_space_constraint(x, pltpu.HBM) for x in operands])


def pick_kernel(order, slots_ref, pieces_ref, out_ref, sem):
    ranks, picks = out_ref.shape[:2]
    slots = slots_ref[...]
    for place, receiver in enumerate(order):
        for s in range(picks):
            piece = pieces_ref.at[ranks - 1 - slots[s + 1, 0, receiver]]
            pltpu.make_async_copy(piece, out_ref.at[place, s], sem).start()
    pltpu.make_async_copy(out_ref, out_ref, sem).wait()


def pick_pieces(slots, pieces, order):
    ranks, *rest = pieces.shape
    return pl.pallas_call(
        functools.partial(pick_kernel, order),
        out_shape=jax.ShapeDtypeStruct((ranks, slots.shape[0] - 1, *rest), pieces.dtype),
        in_specs=[VMEM, VMEM],
        out_specs=ANY,
        scratch_shapes=[pltpu.SemaphoreType.DMA],
        compiler_params=SMALL,
    )(*in_vmem(slots, pieces))


def send_selected(keys, values, slots, ranks, order):
    pieces, slots = pack(keys, values, slots, ranks)
    pieces = pieces.reshape(ranks, *pieces.shape[2:])
    groups = [
        [((g + r) % 2) * ranks + r for r in reversed(range(ranks))] for g in range(2)
    ]
    pieces = lax.all_to_all(
        pieces,
        ("head", "ctx"),
        split_axis=0,
        concat_axis=0,
        axis_index_groups=groups,
        tiled=True,
    )
    return pieces, slots


def send_selected_of_many(keys, values, heads, ranks):
    share = keys.shape[0] // ranks
    pieces = jnp.stack([keys, values]).reshape(2, ranks, share, heads, HD)
    pieces = pieces.transpose(3, 1, 0, 2, 4).reshape(heads * ranks, 2, share, HD)
    pieces = lax.all_to_all(pieces, ("head", "ctx"), split_axis=0, concat_axis=0, tiled=True)
    pieces = pieces.reshape(heads, ranks, 2, share, HD)
    return pieces.transpose(1, 2, 0, 3, 4).reshape(ranks, 2, heads * share, HD)


def units_of(heads_here, size):
    return [(h, begin, begin + size) for h in range(heads_here) for begin in range(0, BLK, size)]


def in_turn(units, score, finish):
    held = [score(*unit) for unit in units[: AHEAD - 1]]
    for i, unit in enumerate(units):
        if i + AHEAD - 1 < len(units):
            held.append(score(*units[i + AHEAD - 1]))
        finish(*unit, held.pop(0))


def near_kernel(
    query_ref, key_ref, value_ref, level_ref, mean_ref, turned, valued
):
    turned[...] = key_ref[...].T
    valued[:, :HD] = value_ref[...]
    valued[:, HD:] = jnp.ones(value_ref.shape, valued.dtype)

    def score(h, begin, end):
        query_rows = query_ref[begin:end, h * HD : (h + 1) * HD]
        scores = jnp.dot(query_rows, turned[:, :end], preferred_element_type=jnp.float32)
        row_ids = lax.broadcasted_iota(jnp.int32, scores.shape, 0) + begin
        col_ids = lax.broadcasted_iota(jnp.int32, scores.shape, 1)
        return jnp.where(row_ids >= col_ids, scores, -jnp.inf)

    def finish(h, begin, end, scores):
        rows = slice(begin, end)
        top = jnp.max(scores, axis=1, keepdims=True)
        weights = jnp.exp2((scores - top) * FACTOR).astype(jnp.bfloat16)
        product = jnp.dot(weights, valued[:end], preferred_element_type=jnp.float32)
        level_ref[h, rows] = top + jnp.log2(product[:, HD:]) / FACTOR
        mean_ref[h, rows] = product[:, :HD] / product[:, HD:]

    in_turn(units_of(query_ref.shape[1] // HD, CHUNK), score, finish)


def attend_near(queries, own_keys, own_values):
    rows, columns = queries.shape
    return pl.pallas_call(
        near_kernel,
        out_shape=[pltpu.VMEM((columns // HD, rows, HD), jnp.float32)] * 2,
        in_specs=[VMEM] * 3,
        out_specs=[VMEM] * 2,
        scratch_shapes=[
            pltpu.VMEM((HD, BLK), jnp.bfloat16),
            pltpu.VMEM((BLK, 2 * HD), jnp.bfloat16),
        ],
        compiler_params=LARGE,
        cost_estimate=pl.CostEstimate(
            flops=4 * columns * rows * BLK, bytes_accessed=4 << 20, transcendentals=0
        ),
    )(*in_vmem(queries, own_keys, own_values))


def far_kernel(
    live_ref, query_ref, far_ref, level_ref, mean_ref, out_ref, turned, valued, ready, sems
):
    heads_here = query_ref.shape[1] // HD
    picks = far_ref.shape[1]

    def leave(h):
        columns = slice(h * HD, (h + 1) * HD)
        return pltpu.make_async_copy(ready.at[h], out_ref.at[:, columns], sems.at[h])

    valued[:, HD:] = jnp.ones((picks * BLK, HD), valued.dtype)

    def attend(slots):
        place = slice(0, len(slots) * BLK)
        for i, s in enumerate(slots):
            part = slice(i * BLK, (i + 1) * BLK)
            turned[:, part] = far_ref[:, s, 0].reshape(BLK, HD).T
            valued[part, :HD] = far_ref[:, s, 1].reshape(BLK, HD)

        def score(h, begin, end):
            query_rows = query_ref[begin:end, h * HD : (h + 1) * HD]
            return jnp.dot(query_rows, turned[:, place], preferred_element_type=jnp.float32)

        def finish(h, begin, end, scores):
            rows = slice(begin, end)
            level = level_ref[h, rows]
            top = jnp.maximum(
                jnp.broadcast_to(jnp.max(scores, axis=1, keepdims=True), level.shape), level
            )
            tiles = [scores[:, i : i + HD] for i in range(0, scores.shape[1], HD)]
            weights = jnp.concatenate(
                [jnp.exp2((tile - top) * FACTOR).astype(jnp.bfloat16) for tile in tiles], axis=1
            )
            product = jnp.dot(weights, valued[place], preferred_element_type=jnp.float32)
            scale = jnp.exp2((level - top) * FACTOR)
            total = product[:, HD:] + scale
            product = product[:, :HD] + mean_ref[h, rows] * scale
            ready[h, rows] = (product / total).astype(ready.dtype)
            if end == BLK:
                leave(h).start()

        in_turn(units_of(heads_here, 2 * CHUNK), score, finish)

    rank = lax.axis_index("ctx")

    @pl.when(rank >= picks)
    def _():
        attend(range(picks))

    @pl.when(rank == 1)
    def _():
        flags = live_ref[...]
        slot = jnp.int32(0)
        for s in range(1, picks):
            slot = jnp.where(flags[0, s] > 0, s, slot)
        attend([slot])

    @pl.when(rank == 0)
    def _():
        for h in range(heads_here):
            ready[h] = mean_ref[h].astype(ready.dtype)
            leave(h).start()

    for h in range(heads_here):
        leave(h).wait()


def attend_far(live, queries, far, near):
    rows, columns = queries.shape
    keys_here = far.shape[1] * BLK
    return pl.pallas_call(
        far_kernel,
        out_shape=jax.ShapeDtypeStruct(queries.shape, queries.dtype),
        in_specs=[VMEM] * 5,
        out_specs=ANY,
        scratch_shapes=[
            pltpu.VMEM((HD, keys_here), jnp.bfloat16),
            pltpu.VMEM((keys_here, 2 * HD), jnp.bfloat16),
            pltpu.VMEM((columns // HD, rows, HD), jnp.bfloat16),
            pltpu.SemaphoreType.DMA((columns // HD,)),
        ],
        compiler_params=LARGE,
    )(*in_vmem(live, queries, far, *near))


def other_head(x):
    return lax.ppermute(x, "head", [(0, 1), (1, 0)])


def own_block(keys, values, heads, head_rank):
    if heads == 2:
        columns = lambda rank: jnp.stack(
            [lax.dynamic_slice_in_dim(x, rank * HD, HD, 1) for x in (keys, values)]
        )
        mine = columns(head_rank)
        came = lax.ppermute(columns(1 - head_rank), "head", [(0, 1), (1, 0)])
        return jnp.where(
            head_rank == 0,
            jnp.concatenate([mine, came], axis=1),
            jnp.concatenate([came, mine], axis=1),
        )
    by_head = jnp.stack([keys, values]).reshape(2, -1, heads, HD).transpose(2, 0, 1, 3)
    own = lax.all_to_all(by_head, "head", split_axis=0, concat_axis=0, tiled=True)
    return own.transpose(1, 0, 2, 3).reshape(2, BLK, HD)


def on_device(heads, ranks, queries, keys, values, selected):
    lists = selected[0]
    picks = lists.shape[1] - 1
    head_rank = lax.axis_index("head")
    ctx_rank = lax.axis_index("ctx")
    share = keys.shape[0] // ranks

    order = [(i + 5 * ranks // 8) % ranks for i in range(ranks)]

    slots = selected.transpose(2, 0, 1)
    plain = heads == 2 and share % 8 == 0 and ranks % 2 == 0
    if plain:
        pieces, slots = send_selected(keys, values, slots, ranks, order)
    else:
        pieces = send_selected_of_many(keys, values, heads, ranks)

    pieces, queries, keys, values = lax.optimization_barrier((pieces, queries, keys, values))

    if plain:
        far = pick_pieces(slots, pieces, order)
    else:
        far = pieces[slots[1:, 0].T[jnp.array(order)]]
    far = lax.all_to_all(
        far, "ctx", split_axis=0, concat_axis=0, axis_index_groups=[order], tiled=True
    )
    if not plain:
        far = far.transpose(1, 2, 0, 3, 4).reshape(1, picks, 2, BLK, HD)

    own = own_block(keys, values, heads, head_rank)
    near = attend_near(queries, own[0], own[1])
    chosen = lax.dynamic_index_in_dim(lists, ctx_rank, 0, keepdims=False)[1:]
    live = (chosen != ctx_rank).astype(jnp.int32)[None]
    return attend_far(live, queries, far, near)


def solution(mesh):
    return jax.shard_map(
        functools.partial(on_device, mesh.shape["head"], mesh.shape["ctx"]),
        mesh=mesh,
        in_specs=(
            P("ctx", "head"),
            P(("ctx", "head"), None),
            P(("ctx", "head"), None),
            P("head", None, None),
        ),
        out_specs=P("ctx", "head"),
        check_vma=False,
    )
```

```python
import functools
import math

import jax
import jax.numpy as jnp
from jax import lax
from jax.experimental import pallas as pl
from jax.experimental.pallas import tpu as pltpu
from jax.sharding import PartitionSpec as P

HD = 128
BLK = 512
CHUNK = 128
AHEAD = 2
FACTOR = math.log2(math.e) / math.sqrt(HD)
SMALL = pltpu.CompilerParams(vmem_limit_bytes=2 * 1024 * 1024)
LARGE = pltpu.CompilerParams(vmem_limit_bytes=12 * 1024 * 1024)
VMEM = pl.BlockSpec(memory_space=pltpu.VMEM)
ANY = pl.BlockSpec(memory_space=pl.ANY)


def in_vmem(*arrays):
    return [pltpu.with_memory_space_constraint(x, pltpu.VMEM) for x in arrays]


def pack_kernel(key_ref, value_ref, slots_ref, out_ref, slots_out, sems, slots_sem):
    group = lax.rem(lax.axis_index("head") + lax.axis_index("ctx"), 2)
    copies = [pltpu.make_async_copy(slots_ref, slots_out, slots_sem)]
    half = key_ref.shape[0] // 2
    for turn in range(2):
        head = lax.rem(group + 1 - turn, 2)
        columns = pl.ds(pl.multiple_of(head * HD, HD), HD)
        for kv, ref in enumerate((key_ref, value_ref)):
            for part in range(2):
                some = slice(part * half, (part + 1) * half)
                copies.append(
                    pltpu.make_async_copy(
                        ref.at[some, :, columns], out_ref.at[some, turn, kv], sems.at[kv, turn, part]
                    )
                )
    for copy in copies:
        copy.start()
    for copy in copies:
        copy.wait()


def pack(keys, values, slots, ranks):
    rows, columns = keys.shape
    pairs = ranks // 2
    operands = [x.reshape(pairs, rows // pairs, columns) for x in (keys, values)] + [slots]
    return pl.pallas_call(
        pack_kernel,
        out_shape=[
            pltpu.VMEM((pairs, 2, 2, rows // pairs, HD), keys.dtype),
            pltpu.VMEM(slots.shape, slots.dtype),
        ],
        in_specs=[ANY] * 3,
        out_specs=[VMEM] * 2,
        scratch_shapes=[pltpu.SemaphoreType.DMA((2, 2, 2)), pltpu.SemaphoreType.DMA],
        compiler_params=SMALL,
    )(*[pltpu.with_memory_space_constraint(x, pltpu.HBM) for x in operands])


def pick_kernel(order, slots_ref, pieces_ref, out_ref, sem):
    ranks, picks = out_ref.shape[:2]
    slots = slots_ref[...]
    for place, receiver in enumerate(order):
        for s in range(picks):
            piece = pieces_ref.at[ranks - 1 - slots[s + 1, 0, receiver]]
            pltpu.make_async_copy(piece, out_ref.at[place, s], sem).start()
    pltpu.make_async_copy(out_ref, out_ref, sem).wait()


def pick_pieces(slots, pieces, order):
    ranks, *rest = pieces.shape
    return pl.pallas_call(
        functools.partial(pick_kernel, order),
        out_shape=jax.ShapeDtypeStruct((ranks, slots.shape[0] - 1, *rest), pieces.dtype),
        in_specs=[VMEM, VMEM],
        out_specs=ANY,
        scratch_shapes=[pltpu.SemaphoreType.DMA],
        compiler_params=SMALL,
    )(*in_vmem(slots, pieces))


def send_selected(keys, values, slots, ranks, order):
    pieces, slots = pack(keys, values, slots, ranks)
    pieces = pieces.reshape(ranks, *pieces.shape[2:])
    groups = [
        [((g + r) % 2) * ranks + r for r in reversed(range(ranks))] for g in range(2)
    ]
    pieces = lax.all_to_all(
        pieces,
        ("head", "ctx"),
        split_axis=0,
        concat_axis=0,
        axis_index_groups=groups,
        tiled=True,
    )
    return pieces, slots


def send_selected_of_many(keys, values, heads, ranks):
    share = keys.shape[0] // ranks
    pieces = jnp.stack([keys, values]).reshape(2, ranks, share, heads, HD)
    pieces = pieces.transpose(3, 1, 0, 2, 4).reshape(heads * ranks, 2, share, HD)
    pieces = lax.all_to_all(pieces, ("head", "ctx"), split_axis=0, concat_axis=0, tiled=True)
    pieces = pieces.reshape(heads, ranks, 2, share, HD)
    return pieces.transpose(1, 2, 0, 3, 4).reshape(ranks, 2, heads * share, HD)


def units_of(heads_here, size):
    return [(h, begin, begin + size) for h in range(heads_here) for begin in range(0, BLK, size)]


def in_turn(units, score, finish):
    held = [score(*unit) for unit in units[: AHEAD - 1]]
    for i, unit in enumerate(units):
        if i + AHEAD - 1 < len(units):
            held.append(score(*units[i + AHEAD - 1]))
        finish(*unit, held.pop(0))


def near_kernel(
    query_ref, key_ref, value_ref, level_ref, mean_ref, turned, valued
):
    turned[...] = key_ref[...].T
    valued[:, :HD] = value_ref[...]
    valued[:, HD:] = jnp.ones(value_ref.shape, valued.dtype)

    def score(h, begin, end):
        query_rows = query_ref[begin:end, h * HD : (h + 1) * HD]
        scores = jnp.dot(query_rows, turned[:, :end], preferred_element_type=jnp.float32)
        row_ids = lax.broadcasted_iota(jnp.int32, scores.shape, 0) + begin
        col_ids = lax.broadcasted_iota(jnp.int32, scores.shape, 1)
        return jnp.where(row_ids >= col_ids, scores, -jnp.inf)

    def finish(h, begin, end, scores):
        rows = slice(begin, end)
        top = jnp.max(scores, axis=1, keepdims=True)
        weights = jnp.exp2((scores - top) * FACTOR).astype(jnp.bfloat16)
        product = jnp.dot(weights, valued[:end], preferred_element_type=jnp.float32)
        level_ref[h, rows] = top + jnp.log2(product[:, HD:]) / FACTOR
        mean_ref[h, rows] = product[:, :HD] / product[:, HD:]

    in_turn(units_of(query_ref.shape[1] // HD, CHUNK), score, finish)


def attend_near(queries, own_keys, own_values):
    rows, columns = queries.shape
    return pl.pallas_call(
        near_kernel,
        out_shape=[pltpu.VMEM((columns // HD, rows, HD), jnp.float32)] * 2,
        in_specs=[VMEM] * 3,
        out_specs=[VMEM] * 2,
        scratch_shapes=[
            pltpu.VMEM((HD, BLK), jnp.bfloat16),
            pltpu.VMEM((BLK, 2 * HD), jnp.bfloat16),
        ],
        compiler_params=LARGE,
        cost_estimate=pl.CostEstimate(
            flops=4 * columns * rows * BLK, bytes_accessed=4 << 20, transcendentals=0
        ),
    )(*in_vmem(queries, own_keys, own_values))


def far_kernel(
    live_ref, query_ref, far_ref, level_ref, mean_ref, out_ref, turned, valued, ready, sems
):
    heads_here = query_ref.shape[1] // HD
    picks = far_ref.shape[1]

    def leave(h):
        columns = slice(h * HD, (h + 1) * HD)
        return pltpu.make_async_copy(ready.at[h], out_ref.at[:, columns], sems.at[h])

    valued[:, HD:] = jnp.ones((picks * BLK, HD), valued.dtype)

    def attend(slots):
        place = slice(0, len(slots) * BLK)
        for i, s in enumerate(slots):
            part = slice(i * BLK, (i + 1) * BLK)
            turned[:, part] = far_ref[:, s, 0].reshape(BLK, HD).T
            valued[part, :HD] = far_ref[:, s, 1].reshape(BLK, HD)

        def score(h, begin, end):
            query_rows = query_ref[begin:end, h * HD : (h + 1) * HD]
            return jnp.dot(query_rows, turned[:, place], preferred_element_type=jnp.float32)

        def finish(h, begin, end, scores):
            rows = slice(begin, end)
            level = level_ref[h, rows]
            top = jnp.maximum(
                jnp.broadcast_to(jnp.max(scores, axis=1, keepdims=True), level.shape), level
            )
            tiles = [scores[:, i : i + HD] for i in range(0, scores.shape[1], HD)]
            weights = jnp.concatenate(
                [jnp.exp2((tile - top) * FACTOR).astype(jnp.bfloat16) for tile in tiles], axis=1
            )
            product = jnp.dot(weights, valued[place], preferred_element_type=jnp.float32)
            scale = jnp.exp2((level - top) * FACTOR)
            total = product[:, HD:] + scale
            product = product[:, :HD] + mean_ref[h, rows] * scale
            ready[h, rows] = (product / total).astype(ready.dtype)
            pltpu.make_async_copy(
                ready.at[h, rows], out_ref.at[rows, h * HD : (h + 1) * HD], sems.at[h]
            ).start()

        in_turn(units_of(heads_here, 2 * CHUNK), score, finish)

    rank = lax.axis_index("ctx")

    @pl.when(rank >= picks)
    def _():
        attend(range(picks))

    @pl.when(rank == 1)
    def _():
        flags = live_ref[...]
        slot = jnp.int32(0)
        for s in range(1, picks):
            slot = jnp.where(flags[0, s] > 0, s, slot)
        attend([slot])

    @pl.when(rank == 0)
    def _():
        for h in range(heads_here):
            ready[h] = mean_ref[h].astype(ready.dtype)
            leave(h).start()

    for h in range(heads_here):
        leave(h).wait()


def attend_far(live, queries, far, near):
    rows, columns = queries.shape
    keys_here = far.shape[1] * BLK
    return pl.pallas_call(
        far_kernel,
        out_shape=jax.ShapeDtypeStruct(queries.shape, queries.dtype),
        in_specs=[VMEM] * 5,
        out_specs=ANY,
        scratch_shapes=[
            pltpu.VMEM((HD, keys_here), jnp.bfloat16),
            pltpu.VMEM((keys_here, 2 * HD), jnp.bfloat16),
            pltpu.VMEM((columns // HD, rows, HD), jnp.bfloat16),
            pltpu.SemaphoreType.DMA((columns // HD,)),
        ],
        compiler_params=LARGE,
    )(*in_vmem(live, queries, far, *near))


def other_head(x):
    return lax.ppermute(x, "head", [(0, 1), (1, 0)])


def own_block(keys, values, heads, head_rank):
    if heads == 2:
        columns = lambda rank: jnp.stack(
            [lax.dynamic_slice_in_dim(x, rank * HD, HD, 1) for x in (keys, values)]
        )
        mine = columns(head_rank)
        came = lax.ppermute(columns(1 - head_rank), "head", [(0, 1), (1, 0)])
        return jnp.where(
            head_rank == 0,
            jnp.concatenate([mine, came], axis=1),
            jnp.concatenate([came, mine], axis=1),
        )
    by_head = jnp.stack([keys, values]).reshape(2, -1, heads, HD).transpose(2, 0, 1, 3)
    own = lax.all_to_all(by_head, "head", split_axis=0, concat_axis=0, tiled=True)
    return own.transpose(1, 0, 2, 3).reshape(2, BLK, HD)


def on_device(heads, ranks, queries, keys, values, selected):
    lists = selected[0]
    picks = lists.shape[1] - 1
    head_rank = lax.axis_index("head")
    ctx_rank = lax.axis_index("ctx")
    share = keys.shape[0] // ranks

    order = [(i + 5 * ranks // 8) % ranks for i in range(ranks)]

    slots = selected.transpose(2, 0, 1)
    plain = heads == 2 and share % 8 == 0 and ranks % 2 == 0
    if plain:
        pieces, slots = send_selected(keys, values, slots, ranks, order)
    else:
        pieces = send_selected_of_many(keys, values, heads, ranks)

    pieces, queries, keys, values = lax.optimization_barrier((pieces, queries, keys, values))

    if plain:
        far = pick_pieces(slots, pieces, order)
    else:
        far = pieces[slots[1:, 0].T[jnp.array(order)]]
    far = lax.all_to_all(
        far, "ctx", split_axis=0, concat_axis=0, axis_index_groups=[order], tiled=True
    )
    if not plain:
        far = far.transpose(1, 2, 0, 3, 4).reshape(1, picks, 2, BLK, HD)

    own = own_block(keys, values, heads, head_rank)
    near = attend_near(queries, own[0], own[1])
    chosen = lax.dynamic_index_in_dim(lists, ctx_rank, 0, keepdims=False)[1:]
    live = (chosen != ctx_rank).astype(jnp.int32)[None]
    return attend_far(live, queries, far, near)


def solution(mesh):
    return jax.shard_map(
        functools.partial(on_device, mesh.shape["head"], mesh.shape["ctx"]),
        mesh=mesh,
        in_specs=(
            P("ctx", "head"),
            P(("ctx", "head"), None),
            P(("ctx", "head"), None),
            P("head", None, None),
        ),
        out_specs=P("ctx", "head"),
        check_vma=False,
    )
```
